256 devices in a mesh: sec: 2 (over x_lo), dom: 128 (over x_hi, y, z, core).
Axes of the slice: x: 4 (x_hi: 2, x_lo: 2; x = x_hi * 2 + x_lo), y: 4, z: 8, core: 2. Of those that a mesh axis runs over, the one named last changes fastest.
Arguments:
- velocity: float32 [256, 3, 32, 32, 128], P(('sec', 'dom')), may hold values from -6 to 6
- first_kernel: bfloat16 [3, 3, 3, 3, 64], replicated, may hold values from -0.625 to 0.625
- norm_gain: float32 [64], replicated, may hold values from 0.5 to 1.5
- second_kernel: bfloat16 [3, 3, 3, 64, 128], replicated, may hold values from -0.15625 to 0.15625
- head_weight: bfloat16 [128, 6], replicated, may hold values from -0.5 to 0.5
- selection: int32 [256, 1], P(('sec', 'dom')), may hold values from 0 to 3
- assignment: int32 [256, 1], replicated, may hold values from 0 to 255, as said below
- target_stress: bfloat16 [256, 1, 3072], P(('sec', 'dom')), may hold values from -6 to 6
Outputs:
- pressure: float32 [256, 32, 32, 128], P(('sec', 'dom'))
- predicted_stress: bfloat16 [256, 1, 3072], P(('sec', 'dom'))
- first_gradient: float32 [3, 3, 3, 3, 64], replicated
- gain_gradient: float32 [64], replicated
- second_gradient: float32 [3, 3, 3, 64, 128], replicated
- head_gradient: float32 [128, 6], replicated
The draws below stay inside these ranges and needn't reach their ends.
Inputs may be any that keep to these rules, and one draw needn't show every extreme that they name: `selection`: local block numbers of one subdomain. `assignment`: every network device is named exactly 1 times in the whole table.
All inputs are finite; a program needn't handle non-finite values.
Results may differ from the reference program's by a relative error of at most 0.011.
Values may be sent and summed in bfloat16 or wider, within the bound.
A program may use at most 128 MiB of HBM per device.

```python
import jax
import jax.numpy as jnp
from jax import lax

CX = 32
CY = 32
CZ = 128
BE = 32
SNAP = 1
OV = 2
SWEEPS = 4
ITERS = 2
C1 = 64
C2 = 128
GY = 4
GZ = 8
GXH = 4
SUBS = 256
NBLK = 4
STRESS = 3072
NX = 256
NY = 128
NZ = 1024
DEVICES = 256


def draw_assignment(key, part):
    key = jax.random.fold_in(key, 11)
    shuffled = jax.random.permutation(key, DEVICES * SNAP)
    return (shuffled // SNAP).reshape(DEVICES, SNAP).astype(jnp.int32)


def set_ends(entries, stream_key, smallest, largest):
    spot = [jax.random.randint(jax.random.fold_in(stream_key, axis), (), 0, length) for axis, length in enumerate(entries.shape)]
    widest = entries.shape.index(max(entries.shape))
    neighbour = spot[:widest] + [(spot[widest] + 1) % entries.shape[widest]] + spot[widest + 1:]
    return entries.at[tuple(spot)].set(smallest).at[tuple(neighbour)].set(largest)


def block_levels(key, shape, split, low, high):
    gain, own = 1.0, jax.random.fold_in(key, 6)
    for axis_at, blocks in split:
        heights = jnp.exp(jax.random.uniform(jax.random.fold_in(own, axis_at), (blocks,), jnp.float32, low / len(split), high / len(split)))
        gain = gain * jnp.repeat(heights, shape[axis_at] // blocks).reshape([-1 if axis == axis_at else 1 for axis in range(len(shape))])
    return gain


def scatter_about(rng, dims, deviation, most, shards=(), kind=jnp.bfloat16):
    loudness = block_levels(rng, dims, shards, -0.22, 0.18) if shards else 1.0
    values = jax.random.normal(rng, dims, jnp.float32) * deviation * loudness
    return jnp.minimum(jnp.maximum(values, -most), most).astype(kind)


def setup_inputs(seed: int = 0) -> dict:
    seeds = jax.random.split(jax.random.key(seed), 9)
    velocity = scatter_about(seeds[0], (SUBS, 3, CX, CY, CZ), 1.0, 6.0, ((0, 256),), jnp.float32)
    first_kernel = scatter_about(seeds[1], (3, 3, 3, 3, C1), 81 ** -0.5, 0.625)
    norm_gain = jnp.clip(1.0 + 0.1 * jax.random.normal(seeds[2], (C1,), jnp.float32), 0.5, 1.5)
    second_kernel = scatter_about(seeds[3], (3, 3, 3, C1, C2), (27 * C1) ** -0.5, 0.15625)
    head_weight = scatter_about(seeds[4], (C2, 6), C2 ** -0.5, 0.5)
    selection = set_ends(jax.random.randint(seeds[5], (SUBS, SNAP), 0, NBLK), jax.random.fold_in(seeds[5], 1), 0, NBLK - 1).astype(jnp.int32)
    assignment = draw_assignment(jax.random.fold_in(seeds[8], 71), 0)
    target_stress = scatter_about(seeds[7], (SUBS, SNAP, STRESS), 1.0, 6.0, ((0, 256),))
    return {"velocity": velocity, "first_kernel": first_kernel, "norm_gain": norm_gain, "second_kernel": second_kernel, "head_weight": head_weight, "selection": selection, "assignment": assignment, "target_stress": target_stress}


NORM_EPS = 1e-05
CONV_LAYOUT = ('NDHWC', 'DHWIO', 'NDHWC')

def conv_layer(inputs, kernel, stride):
    return lax.conv_general_dilated(inputs, kernel, (stride, stride, stride), ((1, 1), (1, 1), (1, 1)), dimension_numbers=CONV_LAYOUT, preferred_element_type=jnp.float32)

def network_loss(weights, batch_rows, targets):
    first_kernel, norm_gain, second_kernel, head_weight = weights
    batch_size = batch_rows.shape[0]
    blocks = batch_rows.reshape(batch_size, 3, BE, BE, BE).transpose(0, 2, 3, 4, 1)
    first_out = conv_layer(blocks, first_kernel, 2)
    chan_mean = lax.optimization_barrier(jnp.mean(first_out, axis=(0, 1, 2, 3)))
    centred = first_out - chan_mean
    variance = lax.optimization_barrier(jnp.mean(centred * centred, axis=(0, 1, 2, 3)))
    normed = centred * (norm_gain * lax.rsqrt(variance + NORM_EPS))
    hidden = jax.nn.silu(normed).astype(jnp.bfloat16)
    second_out = conv_layer(hidden, second_kernel, 2)
    deep_act = jax.nn.silu(second_out).astype(jnp.bfloat16)
    flat_act = deep_act.reshape(-1, deep_act.shape[-1])
    stress = jnp.dot(flat_act, head_weight, preferred_element_type=jnp.float32)
    stress = stress.reshape(batch_size, -1, 6).transpose(0, 2, 1).reshape(batch_size, -1)
    error_vals = stress - targets.astype(jnp.float32)
    loss_value = jnp.sum(error_vals * error_vals) / (2.0 * batch_size)
    return (loss_value, stress)

def pick_blocks(volume, chosen):
    extent_x, extent_y, extent_z = (volume.shape[1], volume.shape[2], volume.shape[3])
    blocks = volume.reshape(3, extent_x // BE, BE, extent_y // BE, BE, extent_z // BE, BE)
    blocks = blocks.transpose(1, 3, 5, 0, 2, 4, 6).reshape(-1, 3 * BE * BE * BE)
    return jnp.take(blocks, chosen, axis=0).astype(jnp.bfloat16)

def neighbours(padded):
    summed = padded[2:, 1:-1, 1:-1] + padded[:-2, 1:-1, 1:-1]
    summed = summed + padded[1:-1, 2:, 1:-1] + padded[1:-1, :-2, 1:-1]
    return summed + padded[1:-1, 1:-1, 2:] + padded[1:-1, 1:-1, :-2]

def operate(padded):
    return 6.0 * padded[1:-1, 1:-1, 1:-1] - neighbours(padded)

def local_solve(window, inside):
    correction = jnp.zeros_like(window)
    for sweep_num in range(SWEEPS):
        correction = inside * (window + neighbours(jnp.pad(correction, 1))) / 6.0
    return correction[OV:-OV, OV:-OV, OV:-OV]

def assemble(blocks):
    return blocks.reshape(2 * GXH, GY, GZ, CX, CY, CZ).transpose(0, 3, 1, 4, 2, 5).reshape(NX, NY, NZ)

def split_blocks(volume):
    return volume.reshape(2 * GXH, CX, GY, CY, GZ, CZ).transpose(0, 2, 4, 1, 3, 5).reshape(SUBS, CX, CY, CZ)

def divergence(parts):
    summed = jnp.zeros(parts.shape[1:], jnp.float32)
    for axis_num in range(3):
        component = parts[axis_num]
        widths = [(0, 0), (0, 0), (0, 0)]
        widths[axis_num] = (1, 0)
        shifted = lax.slice_in_dim(jnp.pad(component, widths), 0, component.shape[axis_num], axis=axis_num)
        summed = summed + (component - shifted)
    return -summed

def reference(velocity, first_kernel, norm_gain, second_kernel, head_weight, selection, assignment, target_stress):
    parts = jnp.stack([assemble(velocity[:, axis_num]) for axis_num in range(3)])
    source = divergence(parts)
    inside = jnp.pad(jnp.ones((NX, NY, NZ), jnp.float32), OV)
    pressure = jnp.zeros((NX, NY, NZ), jnp.float32)
    for round_num in range(ITERS):
        residual = source - operate(jnp.pad(pressure, 1))
        padded = jnp.pad(residual, OV)

        def solve_one(index):
            corner = ((index // (GY * GZ) * CX).astype(jnp.int32), (index // GZ % GY * CY).astype(jnp.int32), (index % GZ * CZ).astype(jnp.int32))
            extent = (CX + 2 * OV, CY + 2 * OV, CZ + 2 * OV)
            window = lax.dynamic_slice(padded, corner, extent)
            within = lax.dynamic_slice(inside, corner, extent)
            return local_solve(window, within)
        corrections = lax.map(solve_one, jnp.arange(SUBS, dtype=jnp.int32))
        pressure = pressure + assemble(corrections)
    snapshots = lax.map(lambda arg_pair: pick_blocks(arg_pair[0], arg_pair[1]), (velocity, selection))
    snapshots = snapshots.reshape(SUBS * SNAP, 3 * BE * BE * BE)
    order = jnp.argsort(assignment.reshape(-1), stable=True).astype(jnp.int32)
    ranks = jnp.argsort(order, stable=True).astype(jnp.int32)
    weights = (first_kernel, norm_gain, second_kernel, head_weight)

    def one_batch(totals, destination):
        rows = lax.dynamic_slice_in_dim(order, (destination * SNAP).astype(jnp.int32), SNAP)
        batch_rows = jnp.take(snapshots, rows, axis=0)
        targets = target_stress[destination]
        loss_value, pullback, stress = jax.vjp(lambda params: network_loss(params, batch_rows, targets), weights, has_aux=True)
        gradients = pullback(jnp.ones_like(loss_value))[0]
        totals = tuple((total_part + grad_part.astype(jnp.float32) for total_part, grad_part in zip(totals, gradients)))
        return (totals, stress.astype(jnp.bfloat16))
    start_totals = tuple((jnp.zeros(weight_part.shape, jnp.float32) for weight_part in weights))
    totals, all_stress = lax.scan(one_batch, start_totals, jnp.arange(SUBS, dtype=jnp.int32))
    flat_stress = all_stress.reshape(SUBS * SNAP, STRESS)
    predicted = jnp.take(flat_stress, ranks, axis=0).reshape(SUBS, SNAP, STRESS)
    return (split_blocks(pressure), predicted, totals[0], totals[1], totals[2], totals[3])
```

```python
import jax
import jax.numpy as jnp
from jax import lax
from jax.sharding import PartitionSpec as P

BE = 32
OV = 2
SWEEPS = 4
ITERS = 2


NORM_EPS = 1e-05
CONV_LAYOUT = ("NDHWC", "DHWIO", "NDHWC")


def shifted_2(x, axis, by):
    devices = lax.axis_size(axis)
    pairs = [(i, i + by) for i in range(devices) if 0 <= i + by < devices]
    return lax.ppermute(x, axis, pairs)


def conv_layer(inputs, kernel, stride):
    return lax.conv_general_dilated(
        inputs,
        kernel,
        (stride, stride, stride),
        ((1, 1), (1, 1), (1, 1)),
        dimension_numbers=CONV_LAYOUT,
        preferred_element_type=jnp.float32,
    )


def network_loss(weights, batch_rows, targets):
    first_kernel, norm_gain, second_kernel, head_weight = weights
    batch_size = batch_rows.shape[0]
    blocks = batch_rows.reshape(batch_size, 3, BE, BE, BE).transpose(0, 2, 3, 4, 1)
    first_out = conv_layer(blocks, first_kernel, 2)
    chan_mean = jnp.mean(first_out, axis=(0, 1, 2, 3))
    centred = first_out - chan_mean
    variance = jnp.mean(centred * centred, axis=(0, 1, 2, 3))
    normed = centred * (norm_gain * lax.rsqrt(variance + NORM_EPS))
    hidden = jax.nn.silu(normed).astype(jnp.bfloat16)
    second_out = conv_layer(hidden, second_kernel, 2)
    deep_act = jax.nn.silu(second_out).astype(jnp.bfloat16)
    flat_act = deep_act.reshape(-1, deep_act.shape[-1])
    stress = jnp.dot(flat_act, head_weight, preferred_element_type=jnp.float32)
    stress = stress.reshape(batch_size, -1, 6).transpose(0, 2, 1).reshape(batch_size, -1)
    error_vals = stress - targets.astype(jnp.float32)
    loss_value = jnp.sum(error_vals * error_vals) / (2.0 * batch_size)
    return (loss_value, stress)


def pick_blocks(volume, chosen):
    extent_x, extent_y, extent_z = (volume.shape[1], volume.shape[2], volume.shape[3])
    blocks = volume.reshape(3, extent_x // BE, BE, extent_y // BE, BE, extent_z // BE, BE)
    blocks = blocks.transpose(1, 3, 5, 0, 2, 4, 6).reshape(-1, 3 * BE * BE * BE)
    return jnp.take(blocks, chosen, axis=0).astype(jnp.bfloat16)


def neighbours(padded):
    summed = padded[2:, 1:-1, 1:-1] + padded[:-2, 1:-1, 1:-1]
    summed = summed + padded[1:-1, 2:, 1:-1] + padded[1:-1, :-2, 1:-1]
    return summed + padded[1:-1, 1:-1, 2:] + padded[1:-1, 1:-1, :-2]


def operate(padded):
    return 6.0 * padded[1:-1, 1:-1, 1:-1] - neighbours(padded)


def local_solve(window, inside):
    correction = jnp.zeros_like(window)
    for sweep_num in range(SWEEPS):
        correction = inside * (window + neighbours(jnp.pad(correction, 1))) / 6.0
    return correction[OV:-OV, OV:-OV, OV:-OV]


def layout():
    dom_count = lax.axis_size("dom")
    span_y = max(2, dom_count // 32)
    span_z = 2 * span_y
    span_x = 2 * dom_count // (span_y * span_z)
    flat_index = lax.axis_index("sec") * dom_count + lax.axis_index("dom")
    coords = (flat_index // (span_y * span_z), flat_index // span_z % span_y, flat_index % span_z)
    return ((span_x, span_y, span_z), (span_y * span_z, span_z, 1), coords)


def from_below(layers, stride, at_start):
    arrived = shifted_2(layers.astype(jnp.bfloat16), ("sec", "dom"), stride).astype(layers.dtype)
    return jnp.where(at_start, jnp.zeros_like(arrived), arrived)


def from_above(layers, stride, at_end):
    arrived = shifted_2(layers.astype(jnp.bfloat16), ("sec", "dom"), -stride).astype(layers.dtype)
    return jnp.where(at_end, jnp.zeros_like(arrived), arrived)


def extend(volume, margin, layout_info):
    counts, strides, coords = layout_info
    for axis_num in range(3):
        extent = volume.shape[axis_num]
        top_layer = lax.slice_in_dim(volume, extent - margin, extent, axis=axis_num)
        bottom_layer = lax.slice_in_dim(volume, 0, margin, axis=axis_num)
        lower_part = from_below(top_layer, strides[axis_num], coords[axis_num] == 0)
        upper_part = from_above(
            bottom_layer, strides[axis_num], coords[axis_num] == counts[axis_num] - 1
        )
        volume = jnp.concatenate([lower_part, volume, upper_part], axis=axis_num)
    return volume


def divergence(volume, layout_info):
    counts, strides, coords = layout_info
    summed = jnp.zeros(volume.shape[1:], jnp.float32)
    for axis_num in range(3):
        component = volume[axis_num]
        extent = component.shape[axis_num]
        edge_layer = lax.slice_in_dim(component, extent - 1, extent, axis=axis_num)
        rim_layer = from_below(edge_layer, strides[axis_num], coords[axis_num] == 0)
        shifted = jnp.concatenate(
            [rim_layer, lax.slice_in_dim(component, 0, extent - 1, axis=axis_num)], axis=axis_num
        )
        summed = summed + (component - shifted)
    return -summed


def inside_mask(extent_shape, layout_info):
    counts, strides, coords = layout_info
    shape_wide = tuple((extent + 2 * OV for extent in extent_shape))
    inside = jnp.ones(shape_wide, jnp.float32)
    for axis_num in range(3):
        position = lax.broadcasted_iota(jnp.int32, shape_wide, axis_num)
        keep_low = (position >= OV) | (coords[axis_num] > 0)
        keep_high = (position < extent_shape[axis_num] + OV) | (
            coords[axis_num] < counts[axis_num] - 1
        )
        inside = inside * (keep_low & keep_high).astype(jnp.float32)
    return inside


def shards(
    velocity,
    first_kernel,
    norm_gain,
    second_kernel,
    head_weight,
    selection,
    assignment,
    target_stress,
):
    layout_info = layout()
    volume = velocity[0]
    source = divergence(volume, layout_info)
    inside = inside_mask(source.shape, layout_info)
    pressure = jnp.zeros_like(source)
    source_wide = extend(source, OV, layout_info)
    for round_num in range(ITERS):
        if round_num == 0:
            window = source_wide
        else:
            residual = source - operate(extend(pressure, 1, layout_info))
            window = extend(residual, OV, layout_info)
        pressure = pressure + local_solve(window, inside)
    chosen = assignment.reshape(-1)[lax.axis_index("sec") * lax.axis_size("dom") + lax.axis_index("dom")]
    every_target = lax.all_gather(target_stress[0, 0], ("sec", "dom"))
    targets = lax.dynamic_slice_in_dim(every_target, chosen, 1, axis=0)
    batch_rows = pick_blocks(volume, selection[0])
    weights = (first_kernel, norm_gain, second_kernel, head_weight)
    loss_value, pullback, stress = jax.vjp(
        lambda params: network_loss(params, batch_rows, targets), weights, has_aux=True
    )
    gradients = pullback(jnp.ones_like(loss_value))[0]
    predicted = stress.astype(jnp.bfloat16)
    summed = lax.psum(
        (
            gradients[0].astype(jnp.float32),
            gradients[1].astype(jnp.float32),
            gradients[2].astype(jnp.float32),
            gradients[3].astype(jnp.float32),
        ),
        ("sec", "dom"),
    )
    return (pressure[None], predicted[None], summed[0], summed[1], summed[2], summed[3])


def solution(mesh):
    placed = (
        P(("sec", "dom"), None, None, None, None),
        P(),
        P(),
        P(),
        P(),
        P(("sec", "dom"), None),
        P(),
        P(("sec", "dom"), None, None),
    )
    return jax.shard_map(
        shards,
        mesh=mesh,
        in_specs=placed,
        out_specs=(
            P(("sec", "dom"), None, None, None),
            P(("sec", "dom"), None, None),
            P(),
            P(),
            P(),
            P(),
        ),
        check_vma=False,
    )
```

```python
import functools

import jax
import jax.numpy as jnp
from jax import lax
from jax.experimental import pallas as pl
from jax.experimental.pallas import tpu as pltpu
from jax.sharding import PartitionSpec as P

F32 = jnp.float32
BF16 = jnp.bfloat16
NORM_EPS = 1e-05
MESH = pl.DeviceIdType.MESH
RANKS = 16
BIG = 112
SMALL = 8
PIECE = 128


def iota(shape, dim):
    return lax.broadcasted_iota(jnp.int32, shape, dim)


def dot(left, right, cl, cr):
    return lax.dot_general(
        left, right, (((cl,), (cr,)), ((), ())), preferred_element_type=F32
    )


def lanes(t, width=128):
    return slice(t * width, (t + 1) * width)


def build_first_weights(sel, w1_ref, wg, table):
    for kx in range(3):
        for kz in range(3):
            rows = []
            for ky in range(3):
                w = w1_ref[kx, ky, kz].astype(F32)
                rows.append(jnp.concatenate([w, w], axis=1))
            for g in range(4):
                mixed = jnp.zeros((3, 128), F32)
                for ky in range(3):
                    mixed = jnp.where(lax.rem(sel + ky, 4) == g, rows[ky], mixed)
                for i in range(3):
                    wg[(kx * 3 + i) * 4 + g, kz : kz + 1, :] = mixed[i : i + 1]
    row = iota((32, 128), 0)
    upper = (iota((32, 128), 1) >= 64).astype(jnp.int32)
    for t in range(8):
        tap = row - 2 * (2 * t + upper) + 1
        masks = [(tap == k).astype(F32) for k in range(3)]

        def fill(c, carry):
            w = wg[c]
            block = masks[0] * w[0:1] + masks[1] * w[1:2] + masks[2] * w[2:3]
            table[pl.ds(pl.multiple_of(c * 32, 32), 32), lanes(t)] = block.astype(BF16)
            return carry

        lax.fori_loop(0, 36, fill, 0)


def build_second_weights(w2_ref, wp):
    for kx in range(3):
        for ky in range(3):
            k = kx * 3 + ky
            wp[k, 0:64, :] = jnp.zeros((64, 128), BF16)
            for kz in range(3):
                wp[k, 64 + kz * 64 : 128 + kz * 64, :] = w2_ref[kx, ky, kz]


def build_rows(sel, vel_ref, mx):
    keep = lax.shift_right_logical(iota((8, 128), 1), 5) == sel
    top = iota((8, 128), 0) == 0
    for i in range(3):
        mx[i, 0, 0] = jnp.zeros((16, 128), BF16)

        def one(x):
            d = [
                jnp.where(keep, vel_ref[0, i, x, pl.ds(o, 8, stride=4), :], 0.0)
                for o in range(4)
            ]
            before = jnp.where(top, 0.0, pltpu.roll(d[3], 1, 0))
            even = before + pltpu.roll(d[0], 32, 1) + pltpu.roll(d[1], 64, 1)
            odd = d[1] + pltpu.roll(d[2], 32, 1) + pltpu.roll(d[3], 64, 1)
            return jnp.concatenate([even, odd], axis=0).astype(BF16)

        def pair(m, carry):
            mx[i, m, 1] = one(2 * m)
            mx[i, m + 1, 0] = one(2 * m + 1)
            return carry

        lax.fori_loop(0, 16, pair, 0)


def first_rows(mx, kx, i):
    if kx == 0:
        part = mx[i, 0:16, 0]
    elif kx == 1:
        part = mx[i, 0:16, 1]
    else:
        part = mx[i, 1:17, 0]
    return part.reshape(256, 128)


def fold_channels(row):
    total = row[:, lanes(0)]
    for t in range(1, 8):
        total = total + row[:, lanes(t)]
    return total + pltpu.roll(total, 64, 1)


def first_layer(mx, table, cen):
    left = jnp.concatenate(
        [first_rows(mx, kx, i) for kx in range(3) for i in range(3)], axis=1
    )
    for t in range(4):
        cen[:, lanes(t, 256)] = dot(left, table[:, lanes(t, 256)], 1, 0)


def normalise(cen, gain_ref):
    total = fold_channels(jnp.sum(cen[...], axis=0, keepdims=True))
    mean = total * (1.0 / 4096.0)
    square = jnp.zeros((1, 128), F32)
    for t in range(8):
        c = cen[:, lanes(t)] - mean
        cen[:, lanes(t)] = c
        square = square + jnp.sum(c * c, axis=0, keepdims=True)
    var = (square + pltpu.roll(square, 64, 1)) * (1.0 / 4096.0)
    gain = gain_ref[0:1, :]
    gain = jnp.concatenate([gain, gain], axis=1)
    return gain, lax.rsqrt(var + NORM_EPS)


def hidden_rows(cen, scale, lhs):
    top = iota((16, 8, 128), 1) == 0
    for k in range(9):
        lhs[k, :, 0:128] = jnp.zeros((64, 128), BF16)
    for t in range(8):
        n = cen[:, lanes(t)] * scale
        h = (n * jax.nn.sigmoid(n)).reshape(16, 2, 8, 128)
        even, odd = h[:, 0], h[:, 1]
        before = jnp.where(top, 0.0, pltpu.roll(odd, 1, 1))
        for ky, plane in ((0, before), (1, even), (2, odd)):
            plane = plane.reshape(8, 2, 8, 128)
            low, high = plane[:, 0], plane[:, 1]
            shifted = jnp.concatenate([jnp.zeros((1, 8, 128), F32), high[:7]], axis=0)
            for kx, part in ((0, shifted), (1, low), (2, high)):
                lhs[kx * 3 + ky, :, lanes(t + 1)] = part.reshape(64, 128).astype(BF16)


def second_rows(lhs, k):
    return jnp.concatenate(
        [lhs[k, :, p * 128 : p * 128 + 256] for p in range(8)], axis=0
    )


def second_layer(lhs, wp):
    out = jnp.zeros((512, 128), F32)
    for k in range(9):
        out = out + dot(second_rows(lhs, k), wp[k], 1, 0)
    return out


def cell_order():
    r, c = iota((512, 512), 0), iota((512, 512), 1)
    same = (lax.shift_right_logical(c, 3) == lax.bitwise_and(r, 63)) & (
        lax.bitwise_and(c, 7) == lax.shift_right_logical(r, 6)
    )
    return same.astype(F32).astype(BF16)


def target_rows(pieces):
    row = iota((512, 16), 0)
    which = lax.shift_right_logical(lax.bitwise_and(row, 63), 2)
    pick = (which == iota((512, 16), 1)).astype(F32).astype(BF16)
    spread = dot(pick, pieces.astype(BF16), 1, 0)
    row, lane = iota((512, 256), 0), iota((512, 256), 1)
    cell = lax.bitwise_and(row, 3) * 8 + lax.shift_right_logical(row, 6)
    kept = jnp.where(lax.bitwise_and(lane, 31) == cell, spread, 0.0).astype(BF16)
    r, c = iota((256, 128), 0), iota((256, 128), 1)
    collect = (lax.shift_right_logical(r, 5) == c).astype(F32).astype(BF16)
    return dot(kept, collect, 1, 0)


def second_gradient(lhs, dout, gb):
    for k in range(9):
        grad = dot(second_rows(lhs, k), dout, 0, 0)
        gb[k * 192 : (k + 1) * 192, :] = grad[64:256].astype(BF16)


def hidden_gradient(dout, wp, back):
    for k in range(9):
        back[k] = dot(dout, wp[k], 1, 1).astype(F32)


def norm_backward(back, cen, gain, rstd, dn):
    scale = gain * rstd
    bottom = iota((8, 8, 128), 1) == 7
    sums = jnp.zeros((1, 128), F32)
    products = jnp.zeros((1, 128), F32)
    for t in range(8):
        planes = []
        for k in range(9):
            part = back[k, t * 64 : (t + 1) * 64, 128:256]
            if t < 7:
                part = part + back[k, (t + 1) * 64 : (t + 2) * 64, 0:128]
            planes.append(part.reshape(8, 8, 128))
        by_kx = []
        for kx in range(3):
            before = jnp.where(bottom, 0.0, pltpu.roll(planes[kx * 3], 7, 1))
            by_kx.append((planes[kx * 3 + 1], planes[kx * 3 + 2] + before))
        parts = []
        for q in range(2):
            moved = jnp.concatenate(
                [by_kx[0][q][1:], jnp.zeros((1, 8, 128), F32)], axis=0
            )
            parts.append((by_kx[1][q], by_kx[2][q] + moved))
        dh = jnp.stack(
            [
                jnp.stack([parts[0][0], parts[1][0]], axis=1),
                jnp.stack([parts[0][1], parts[1][1]], axis=1),
            ],
            axis=1,
        ).reshape(256, 128)
        dh = dh.astype(BF16).astype(F32)
        c = cen[:, lanes(t)]
        n = c * scale
        s = jax.nn.sigmoid(n)
        d = dh * (s * (1.0 + n * (1.0 - s)))
        dn[:, lanes(t)] = d
        sums = sums + jnp.sum(d, axis=0, keepdims=True)
        products = products + jnp.sum(d * c, axis=0, keepdims=True)
    sums = (sums + pltpu.roll(sums, 64, 1)) * (1.0 / 4096.0)
    products = products + pltpu.roll(products, 64, 1)
    slope = products * (rstd * rstd * (1.0 / 4096.0))
    for t in range(8):
        d = dn[:, lanes(t)]
        dn[:, lanes(t)] = scale * (d - sums - cen[:, lanes(t)] * slope)
    return products * rstd


def first_gradient(sel, mx, dn, gs):
    right = dn[...].astype(BF16)
    row = iota((128, 128), 0)
    z = lax.bitwise_and(row, 31)
    upper = (iota((128, 128), 1) >= 64).astype(jnp.int32)
    for kx in range(3):
        for i in range(3):
            full = dot(first_rows(mx, kx, i), right, 0, 0)
            for kz in range(3):
                total = jnp.zeros((128, 128), F32)
                for t in range(8):
                    tap = z - 2 * (2 * t + upper) + 1
                    total = total + jnp.where(tap == kz, full[:, lanes(t)], 0.0)
                total = jnp.sum(total.reshape(4, 32, 128), axis=1)
                total = total + pltpu.roll(total, 64, 1)
                for ky in range(3):
                    value = jnp.zeros((1, 128), F32)
                    for g in range(4):
                        value = jnp.where(
                            lax.rem(sel + ky, 4) == g, total[g : g + 1], value
                        )
                    at = ((kx * 3 + ky) * 3 + kz) * 3 + i
                    gs[at : at + 1, :] = value


def cell_masks(coords):
    _, by, bz = coords
    y, z = iota((40, 256), 0), iota((40, 256), 1)
    in_y = (y < 32) | ((y < 34) & (by < 3)) | ((y >= 38) & (by > 0))
    in_z = (z < 128) | ((z < 130) & (bz < 7)) | ((z >= 254) & (bz > 0))
    return jnp.where(in_y & in_z, 1.0 / 6.0, 0.0).astype(F32)


def divergence(vel_ref, rim_x, rim_y, rim_z, flags, window):
    first_row = iota((32, 128), 0) == 0
    first_lane = iota((32, 128), 1) == 0

    def layer(x, before):
        ux, uy, uz = vel_ref[0, 0, x], vel_ref[0, 1, x], vel_ref[0, 2, x]
        y_rim = rim_y[pl.ds(x, 1), :] * flags[2]
        y_before = jnp.where(first_row, y_rim, pltpu.roll(uy, 1, 0))
        z_rim = pltpu.roll(rim_z[...], 128 - x if not isinstance(x, int) else 0, 1) * flags[4]
        z_before = jnp.where(first_lane, z_rim, pltpu.roll(uz, 1, 1))
        total = (ux - before) + (uy - y_before) + (uz - z_before)
        window[x + 2, 0:32, 0:128] = -total

    layer(0, rim_x[...] * flags[0])

    def step(x, carry):
        layer(x, vel_ref[0, 0, x - 1])
        return carry

    lax.fori_loop(1, 32, step, 0)


def pack_rim_z(vel_ref, send):
    lane = iota((32, 128), 1)
    packed = jnp.zeros((32, 128), F32)
    for x in range(32):
        moved = pltpu.roll(vel_ref[0, 2, x], (x + 1) % 128, 1)
        packed = jnp.where(lane == x, moved, packed)
    send[...] = packed


def pack_y(field, count, h, w, send):
    sub = iota((8, 128), 0)
    per = 8 // w
    for m in range(count // per):
        high = jnp.zeros((8, 128), F32)
        low = jnp.zeros((8, 128), F32)
        for j in range(per):
            x = m * per + j
            here = (sub >= j * w) & (sub < j * w + w)
            top = pltpu.roll(field[x, 24:32, 0:128], (j * w - (8 - h)) % 8, 0)
            bottom = field[x, 0:8, 0:128]
            if j:
                bottom = pltpu.roll(bottom, j * w, 0)
            high = jnp.where(here, top, high)
            low = jnp.where(here, bottom, low)
        send[0, m] = high
        send[1, m] = low


def unpack_y(field, count, h, w, got, flags):
    sub = iota((8, 128), 0)
    per = 8 // w
    for m in range(count // per):
        below, above = got[0, m] * flags[2], got[1, m] * flags[3]
        for j in range(per):
            lower = pltpu.roll(below, (8 - h - j * w) % 8, 0)
            upper = pltpu.roll(above, (-j * w) % 8, 0) if j else above
            field[m * per + j, 32:40, 0:128] = jnp.where(
                sub < h, upper, jnp.where(sub >= 8 - h, lower, 0.0)
            )


def pack_z(field, count, h, send):
    lane = iota((40, 128), 1)
    high = jnp.zeros((40, 128), F32)
    low = jnp.zeros((40, 128), F32)
    for x in range(count):
        here = (lane >= x * h) & (lane < x * h + h)
        own = field[x, :, 0:128]
        high = jnp.where(here, pltpu.roll(own, (x * h + h) % 128, 1), high)
        low = jnp.where(here, pltpu.roll(own, x * h, 1) if x else own, low)
    send[0] = high
    send[1] = low


def unpack_z(field, count, h, got, flags):
    lane = iota((40, 128), 1)
    below, above = got[0] * flags[4], got[1] * flags[5]
    for x in range(count):
        lower = pltpu.roll(below, (128 - h - x * h) % 128, 1)
        upper = pltpu.roll(above, (-x * h) % 128, 1) if x else above
        field[x, :, 128:256] = jnp.where(
            lane < h, upper, jnp.where(lane >= 128 - h, lower, 0.0)
        )


def neighbours(field, at):
    own = field[at]
    across = field[at - 1] + field[at + 1]
    along = pltpu.roll(own, 1, 0) + pltpu.roll(own, 39, 0)
    return own, across + along + pltpu.roll(own, 1, 1) + pltpu.roll(own, 255, 1)


def local_solve(window, mask, za, zb, flags, pressure, emit):
    def inside(xi):
        return jnp.where(xi < 2, flags[0], jnp.where(xi > 33, flags[1], 1.0))

    for z in (za, zb):
        z[0] = jnp.zeros((40, 256), F32)
        z[37] = jnp.zeros((40, 256), F32)

    def first(xi, carry):
        w = window[xi]
        if pressure is not None:
            own, around = neighbours(pressure, xi + 1)
            w = w - (6.0 * own - around)
            window[xi] = w
        za[xi + 1] = w * (mask[...] * inside(xi))
        return carry

    def sweep(source, target):
        def step(xi, carry):
            _, around = neighbours(source, xi + 1)
            target[xi + 1] = (window[xi] + around) * (mask[...] * inside(xi))
            return carry

        return step

    def last(xi, carry):
        _, around = neighbours(za, xi + 1)
        z = (window[xi] + around) * mask[...]
        emit(xi, z[0:32, 0:128])
        return carry

    lax.fori_loop(0, 36, first, 0)
    lax.fori_loop(0, 36, sweep(za, zb), 0)
    lax.fori_loop(1, 35, sweep(zb, za), 0)
    lax.fori_loop(2, 34, last, 0)


SCRATCH = dict(
    wg=((36, 8, 128), F32),
    table=((1152, 1024), BF16),
    mx=((3, 17, 2, 16, 128), BF16),
    cen=((256, 1024), F32),
    lhs=((9, 64, 1152), BF16),
    wp=((9, 256, 128), BF16),
    hp=((128, 128), BF16),
    back=((9, 512, 256), F32),
    dn=((256, 1024), F32),
    order=((512, 512), BF16),
    t1=((RANKS, 1, 256), F32),
    t2=((RANKS, RANKS, 1, 256), F32),
    stage=((RANKS, 1, 256), F32),
    t3=((RANKS, 1, 256), F32),
    pieces=((RANKS, 256), F32),
    gb=((RANKS * BIG, 128), BF16),
    gs=((RANKS * SMALL, 128), F32),
    r1=((RANKS, BIG, 128), BF16),
    r1s=((RANKS, SMALL, 128), F32),
    part=((RANKS, 8, 128), F32),
    r2=((RANKS, 8, 128), F32),
    whole=((RANKS, 8, 128), F32),
    gathered=((RANKS, PIECE, 128), BF16),
    rim_x=((32, 128), F32),
    rim_y=((32, 128), F32),
    rim_z=((32, 128), F32),
    rim_ys=((32, 128), F32),
    rim_zs=((32, 128), F32),
    window=((36, 40, 256), F32),
    press=((38, 40, 256), F32),
    za=((38, 40, 256), F32),
    zb=((38, 40, 256), F32),
    mask=((40, 256), F32),
    wys=((2, 9, 8, 128), F32),
    wyr=((2, 9, 8, 128), F32),
    wzs=((2, 40, 128), F32),
    wzr=((2, 40, 128), F32),
    pys=((2, 19, 8, 128), F32),
    pyr=((2, 19, 8, 128), F32),
    pzs=((2, 40, 128), F32),
    pzr=((2, 40, 128), F32),
)
GROUP_STEPS = ("t1", "t2", "t3", "g1", "g1s", "g2", "g3", "g4")
HALO_STEPS = ("rim", "wx", "wy", "wz", "px", "py", "pz")
SEMAPHORES = 16 * len(GROUP_STEPS) + 3 * len(HALO_STEPS)


def kernel(*refs):
    (sel_ref, asg_ref, vel_ref, w1_ref, gain_ref, w2_ref, head_ref, target_ref) = refs[:8]
    pressure_ref, pred_ref, grad_ref = refs[8:11]
    s = dict(zip(SCRATCH, refs[11 : 11 + len(SCRATCH)]))
    send_sem, recv_sem = refs[11 + len(SCRATCH) :]

    me = lax.axis_index("sec") * 128 + lax.axis_index("dom")
    a, b = lax.div(me, 16), lax.rem(me, 16)
    coords = (lax.div(me, 32), lax.rem(lax.div(me, 8), 4), lax.rem(me, 8))
    bx, by, bz = coords
    flags = [
        jnp.where(cond, 1.0, 0.0).astype(F32)
        for cond in (bx > 0, bx < 7, by > 0, by < 3, bz > 0, bz < 7)
    ]

    def device(f):
        return (lax.div(f, 128), lax.rem(f, 128))

    def box(x, y, z):
        return device(lax.rem(x + 8, 8) * 32 + lax.rem(y + 4, 4) * 8 + lax.rem(z + 8, 8))

    above = [box(bx + 1, by, bz), box(bx, by + 1, bz), box(bx, by, bz + 1)]
    below = [box(bx - 1, by, bz), box(bx, by - 1, bz), box(bx, by, bz - 1)]
    a_ranks = [None] + [lax.rem(a + j, RANKS) for j in range(1, RANKS)]
    b_ranks = [None] + [lax.rem(b + j, RANKS) for j in range(1, RANKS)]
    a_peers = [None] + [device(a_ranks[j] * 16 + b) for j in range(1, RANKS)]
    b_peers = [None] + [device(a * 16 + b_ranks[j]) for j in range(1, RANKS)]

    barrier = pltpu.get_barrier_semaphore()
    everyone = a_peers[1:] + b_peers[1:] + above + below
    for other in everyone:
        pl.semaphore_signal(barrier, inc=1, device_id=other, device_id_type=MESH)

    started = []
    flights = {}

    def start(step, at, source, target, other):
        base = (
            GROUP_STEPS.index(step) * 16
            if step in GROUP_STEPS
            else 16 * len(GROUP_STEPS) + 3 * HALO_STEPS.index(step)
        )
        copy = pltpu.make_async_remote_copy(
            src_ref=source,
            dst_ref=target,
            send_sem=send_sem.at[base + at],
            recv_sem=recv_sem.at[base + at],
            device_id=other,
            device_id_type=MESH,
        )
        copy.start()
        started.append(copy)
        flights.setdefault(step, []).append(copy)

    def arrive(step, sent=False):
        for copy in flights[step]:
            copy.wait_recv()
            if sent:
                copy.wait_send()
                started[:] = [other for other in started if other is not copy]

    sel = sel_ref[0, 0]
    build_first_weights(sel, w1_ref, s["wg"], s["table"])
    build_second_weights(w2_ref, s["wp"])
    s["hp"][...] = jnp.zeros((128, 128), BF16)
    s["hp"][:, 0:6] = head_ref[...]
    s["mask"][...] = cell_masks(coords)
    pack_rim_z(vel_ref, s["rim_zs"])
    s["rim_ys"][...] = vel_ref[0, 1, :, 31, :]

    pl.semaphore_wait(barrier, len(everyone))

    for j in range(1, RANKS):
        start("t1", j, target_ref.at[a_ranks[j]], s["t1"].at[a], a_peers[j])
    start("rim", 0, vel_ref.at[0, 0, 31], s["rim_x"], above[0])
    start("rim", 1, s["rim_ys"], s["rim_y"], above[1])
    start("rim", 2, s["rim_zs"], s["rim_z"], above[2])
    s["t1"][a] = target_ref[a]

    build_rows(sel, vel_ref, s["mx"])
    arrive("t1")
    for j in range(1, RANKS):
        start("t2", j, s["t1"], s["t2"].at[b], b_peers[j])
    s["t2"][b] = s["t1"][...]
    first_layer(s["mx"], s["table"], s["cen"])
    arrive("rim")
    window = s["window"]
    divergence(vel_ref, s["rim_x"], s["rim_y"], s["rim_z"], flags, window)
    own = (slice(0, 32), slice(0, 128))
    start("wx", 0, window.at[32:34, 0:32, 0:128], window.at[0:2, 0:32, 0:128], above[0])
    start("wx", 1, window.at[2:4, 0:32, 0:128], window.at[34:36, 0:32, 0:128], below[0])
    gain, rstd = normalise(s["cen"], gain_ref)
    arrive("t2")
    for q in range(RANKS):
        wanted = asg_ref[q * 16 + b]
        s["stage"][q] = s["t2"][lax.rem(wanted, 16), lax.div(wanted, 16)]
    for j in range(1, RANKS):
        start("t3", j, s["stage"].at[a_ranks[j]], s["t3"].at[a], a_peers[j])
    s["t3"][a] = s["stage"][a]
    hidden_rows(s["cen"], gain * rstd, s["lhs"])
    arrive("wx", True)
    pack_y(window, 36, 2, 2, s["wys"])
    start("wy", 0, s["wys"].at[0], s["wyr"].at[0], above[1])
    start("wy", 1, s["wys"].at[1], s["wyr"].at[1], below[1])

    out = second_layer(s["lhs"], s["wp"])
    sig = jax.nn.sigmoid(out)
    deep = (out * sig).astype(BF16)
    slope = sig * (1.0 + out * (1.0 - sig))
    stress = dot(deep, s["hp"][...], 1, 0)
    arrive("t3")
    for q in range(RANKS):
        s["pieces"][q : q + 1, :] = s["t3"][q]
    error = (stress - target_rows(s["pieces"][...])).astype(BF16)
    dout = dot(error, s["hp"][...], 1, 1).astype(BF16).astype(F32) * slope
    dout = dout.astype(BF16)

    s["gb"][1728:1792, :] = jnp.zeros((64, 128), BF16)
    second_gradient(s["lhs"], dout, s["gb"])
    for j in range(1, RANKS):
        rows = pl.ds(pl.multiple_of(a_ranks[j] * BIG, 16), BIG)
        start("g1", j, s["gb"].at[rows], s["r1"].at[j], a_peers[j])

    arrive("wy")
    unpack_y(window, 36, 2, 2, s["wyr"], flags)
    pack_z(window, 36, 2, s["wzs"])
    start("wz", 0, s["wzs"].at[0], s["wzr"].at[0], above[2])
    start("wz", 1, s["wzs"].at[1], s["wzr"].at[1], below[2])

    gs = s["gs"]
    gs[...] = jnp.zeros((128, 128), F32)
    gs[82:88, :] = dot(error, deep, 0, 0)[0:6]
    hidden_gradient(dout, s["wp"], s["back"])
    gs[81:82, :] = norm_backward(s["back"], s["cen"], gain, rstd, s["dn"])
    first_gradient(sel, s["mx"], s["dn"], gs)
    for j in range(1, RANKS):
        rows = pl.ds(pl.multiple_of(a_ranks[j] * SMALL, 8), SMALL)
        start("g1s", j, gs.at[rows], s["r1s"].at[j], a_peers[j])
    pred_ref[...] = dot(stress.astype(BF16), cell_order(), 0, 0)[0:8]

    arrive("wz")
    unpack_z(window, 36, 2, s["wzr"], flags)
    press = s["press"]

    def keep(xi, z):
        press[xi + 1, 0:32, 0:128] = z

    local_solve(window, s["mask"], s["za"], s["zb"], flags, None, keep)
    start("px", 0, press.at[32:35, 0:32, 0:128], press.at[0:3, 0:32, 0:128], above[0])
    start("px", 1, press.at[3:6, 0:32, 0:128], press.at[35:38, 0:32, 0:128], below[0])

    arrive("g1")
    arrive("g1s")
    rows = pl.ds(pl.multiple_of(a * BIG, 16), BIG)
    big = s["gb"][rows, :].astype(F32)
    small = gs[pl.ds(pl.multiple_of(a * SMALL, 8), SMALL), :]
    for j in range(1, RANKS):
        big = big + s["r1"][j].astype(F32)
        small = small + s["r1s"][j]
    part = s["part"]
    part[0:14] = big.reshape(14, 8, 128)
    part[14] = small
    part[15] = jnp.zeros((8, 128), F32)
    for j in range(1, RANKS):
        start("g2", j, part.at[b_ranks[j]], s["r2"].at[j], b_peers[j])

    arrive("px", True)
    press[0:3, 0:32, 0:128] = press[0:3, 0:32, 0:128] * flags[0]
    press[35:38, 0:32, 0:128] = press[35:38, 0:32, 0:128] * flags[1]
    pack_y(press, 38, 3, 4, s["pys"])
    start("py", 0, s["pys"].at[0], s["pyr"].at[0], above[1])
    start("py", 1, s["pys"].at[1], s["pyr"].at[1], below[1])

    arrive("g2")
    total = part[b]
    for j in range(1, RANKS):
        total = total + s["r2"][j]
    s["whole"][b] = total
    for j in range(1, RANKS):
        start("g3", j, s["whole"].at[b], s["whole"].at[b], b_peers[j])

    arrive("py")
    unpack_y(press, 38, 3, 4, s["pyr"], flags)
    pack_z(press, 38, 3, s["pzs"])
    start("pz", 0, s["pzs"].at[0], s["pzr"].at[0], above[2])
    start("pz", 1, s["pzs"].at[1], s["pzr"].at[1], below[2])

    arrive("g3")
    gathered = s["gathered"]
    gathered[a] = s["whole"][...].reshape(PIECE, 128).astype(BF16)
    for j in range(1, RANKS):
        start("g4", j, gathered.at[a], gathered.at[a], a_peers[j])

    arrive("pz")
    unpack_z(press, 38, 3, s["pzr"], flags)

    def finish(xi, z):
        pressure_ref[xi - 2] = press[xi + 1, 0:32, 0:128] + z

    local_solve(window, s["mask"], s["za"], s["zb"], flags, press, finish)
    arrive("g4")
    grad_ref[...] = gathered[...]
    for copy in started:
        copy.wait_send()


def shards(
    velocity,
    first_kernel,
    norm_gain,
    second_kernel,
    head_weight,
    selection,
    assignment,
    target_stress,
):
    pieces = target_stress.reshape(6, 16, 32).transpose(1, 0, 2).reshape(16, 192)
    pieces = jnp.pad(pieces.astype(F32), ((0, 0), (0, 64))).reshape(16, 1, 256)
    vmem = pl.BlockSpec(memory_space=pltpu.VMEM)
    smem = pl.BlockSpec(memory_space=pltpu.SMEM)
    pressure, stress, grads = pl.pallas_call(
        kernel,
        out_shape=[
            jax.ShapeDtypeStruct((32, 32, 128), F32),
            jax.ShapeDtypeStruct((8, 512), F32),
            jax.ShapeDtypeStruct((RANKS, PIECE, 128), BF16),
        ],
        in_specs=[smem, smem] + [vmem] * 6,
        out_specs=[vmem] * 3,
        scratch_shapes=[pltpu.VMEM(shape, kind) for shape, kind in SCRATCH.values()]
        + [pltpu.SemaphoreType.DMA((SEMAPHORES,))] * 2,
        compiler_params=pltpu.CompilerParams(
            collective_id=0, has_side_effects=True, vmem_limit_bytes=56 << 20
        ),
    )(
        selection,
        assignment.reshape(-1),
        velocity,
        first_kernel,
        norm_gain.reshape(1, 64),
        second_kernel,
        head_weight,
        pieces,
    )
    predicted = stress[:6].astype(BF16).reshape(1, 1, 3072)
    second = grads[:, :BIG].reshape(RANKS * BIG, 128)[:1728].astype(F32)
    rest = grads[:, BIG : BIG + SMALL].reshape(RANKS * SMALL, 128).astype(F32)
    return (
        pressure[None],
        predicted,
        rest[:81, :64].reshape(3, 3, 3, 3, 64),
        rest[81, :64],
        second.reshape(3, 3, 3, 64, 128),
        rest[82:88].T,
    )


def solution(mesh):
    placed = (
        P(("sec", "dom"), None, None, None, None),
        P(),
        P(),
        P(),
        P(),
        P(("sec", "dom"), None),
        P(),
        P(("sec", "dom"), None, None),
    )
    return jax.shard_map(
        shards,
        mesh=mesh,
        in_specs=placed,
        out_specs=(
            P(("sec", "dom"), None, None, None),
            P(("sec", "dom"), None, None),
            P(),
            P(),
            P(),
            P(),
        ),
        check_vma=False,
    )
```

```python
import jax
import jax.numpy as jnp
from jax import lax
from jax.experimental import pallas as pl
from jax.experimental.pallas import tpu as pltpu
from jax.sharding import PartitionSpec as P

F32 = jnp.float32
BF16 = jnp.bfloat16
NORM_EPS = 1e-05
MESH = pl.DeviceIdType.MESH
RANKS = 16
BIG = 112
SMALL = 8


def iota(shape, dim):
    return lax.broadcasted_iota(jnp.int32, shape, dim)


def dot(left, right, cl, cr):
    return lax.dot_general(
        left, right, (((cl,), (cr,)), ((), ())), preferred_element_type=F32
    )


def lanes(t, width=128):
    return slice(t * width, (t + 1) * width)


def build_first_weights(sel, w1_ref, wg, table):
    for kx in range(3):
        for kz in range(3):
            rows = []
            for ky in range(3):
                w = w1_ref[kx, ky, kz].astype(F32)
                rows.append(jnp.concatenate([w, w], axis=1))
            for g in range(4):
                mixed = jnp.zeros((3, 128), F32)
                for ky in range(3):
                    mixed = jnp.where(lax.rem(sel + ky, 4) == g, rows[ky], mixed)
                for i in range(3):
                    wg[(kx * 3 + i) * 4 + g, kz : kz + 1, :] = mixed[i : i + 1]
    row = iota((32, 128), 0)
    upper = (iota((32, 128), 1) >= 64).astype(jnp.int32)
    for t in range(8):
        tap = row - 2 * (2 * t + upper) + 1
        masks = [(tap == k).astype(F32) for k in range(3)]

        for c in range(0, 36, 12):
            w = wg[c : c + 12]
            block = sum(masks[k][None] * w[:, k : k + 1, :] for k in range(3))
            table[c : c + 12, :, lanes(t)] = block.astype(BF16)


def build_second_weights(w2_ref, wp):
    for kx in range(3):
        for ky in range(3):
            k = kx * 3 + ky
            wp[k, 0:64, :] = jnp.zeros((64, 128), BF16)
            for kz in range(3):
                wp[k, 64 + kz * 64 : 128 + kz * 64, :] = w2_ref[kx, ky, kz]


def build_rows(sel, vel_ref, mx):
    keep = lax.shift_right_logical(iota((8, 8, 128), 2), 5) == sel
    top = iota((8, 8, 128), 1) == 0
    for i in range(3):
        mx[i, 0, 0] = jnp.zeros((16, 128), BF16)
        for m in range(0, 16, 4):
            d = []
            for o in range(4):
                rows = vel_ref[0, i, 2 * m : 2 * m + 8, pl.ds(o, 8, stride=4), :]
                d.append(jnp.where(keep, rows, 0.0))
            before = jnp.where(top, 0.0, pltpu.roll(d[3], 1, 1))
            even = before + pltpu.roll(d[0], 32, 2) + pltpu.roll(d[1], 64, 2)
            odd = d[1] + pltpu.roll(d[2], 32, 2) + pltpu.roll(d[3], 64, 2)
            both = jnp.concatenate([even, odd], axis=1).astype(BF16)
            both = both.reshape(4, 2, 16, 128)
            mx[i, m : m + 4, 1] = both[:, 0]
            mx[i, m + 1 : m + 5, 0] = both[:, 1]


def first_rows(mx, kx, i):
    if kx == 0:
        part = mx[i, 0:16, 0]
    elif kx == 1:
        part = mx[i, 0:16, 1]
    else:
        part = mx[i, 1:17, 0]
    return part.reshape(256, 128)


def fold_channels(row):
    total = row[:, lanes(0)]
    for t in range(1, 8):
        total = total + row[:, lanes(t)]
    return total + pltpu.roll(total, 64, 1)


def first_layer(mx, table, cen):
    left = jnp.concatenate(
        [first_rows(mx, kx, i) for kx in range(3) for i in range(3)], axis=1
    )
    for t in range(4):
        right = table[:, :, lanes(t, 256)].reshape(1152, 256)
        cen[:, lanes(t, 256)] = dot(left, right, 1, 0)


def normalise(cen, gain_ref):
    total = fold_channels(jnp.sum(cen[...], axis=0, keepdims=True))
    mean = total * (1.0 / 4096.0)
    square = jnp.zeros((1, 128), F32)
    for t in range(8):
        c = cen[:, lanes(t)] - mean
        cen[:, lanes(t)] = c
        square = square + jnp.sum(c * c, axis=0, keepdims=True)
    var = (square + pltpu.roll(square, 64, 1)) * (1.0 / 4096.0)
    gain = gain_ref[0:1, :]
    gain = jnp.concatenate([gain, gain], axis=1)
    return gain, lax.rsqrt(var + NORM_EPS)


def hidden_rows(cen, scale, lhs):
    top = iota((16, 8, 128), 1) == 0
    for k in range(9):
        lhs[k, :, 0:128] = jnp.zeros((64, 128), BF16)
    for t in range(8):
        n = cen[:, lanes(t)] * scale
        h = (n * jax.nn.sigmoid(n)).reshape(16, 2, 8, 128)
        even, odd = h[:, 0], h[:, 1]
        before = jnp.where(top, 0.0, pltpu.roll(odd, 1, 1))
        for ky, plane in ((0, before), (1, even), (2, odd)):
            plane = plane.reshape(8, 2, 8, 128)
            low, high = plane[:, 0], plane[:, 1]
            shifted = jnp.concatenate([jnp.zeros((1, 8, 128), F32), high[:7]], axis=0)
            for kx, part in ((0, shifted), (1, low), (2, high)):
                lhs[kx * 3 + ky, :, lanes(t + 1)] = part.reshape(64, 128).astype(BF16)


def second_rows(lhs, k):
    return jnp.concatenate(
        [lhs[k, :, p * 128 : p * 128 + 256] for p in range(8)], axis=0
    )


def second_layer(lhs, wp):
    out = jnp.zeros((512, 128), F32)
    for k in range(9):
        out = out + dot(second_rows(lhs, k), wp[k], 1, 0)
    return out


def cell_order():
    r, c = iota((512, 512), 0), iota((512, 512), 1)
    same = (lax.shift_right_logical(c, 3) == lax.bitwise_and(r, 63)) & (
        lax.bitwise_and(c, 7) == lax.shift_right_logical(r, 6)
    )
    return same.astype(F32).astype(BF16)


def target_rows(flat, wide):
    wide[...] = jnp.zeros((8, 768), F32)
    for k in range(6):
        wide[0:4, lanes(k)] = flat[4 * k : 4 * k + 4]
    row = iota((512, 8), 0)
    which = lax.bitwise_and(lax.shift_right_logical(row, 4), 3)
    pick = (which == iota((512, 8), 1)).astype(F32).astype(BF16)
    spread = dot(pick, wide[...].astype(BF16), 1, 0)
    row, lane = iota((512, 768), 0), iota((512, 768), 1)
    cell = (
        lax.bitwise_and(lax.shift_right_logical(row, 3), 1) * 64
        + lax.bitwise_and(row, 7) * 8
        + lax.shift_right_logical(row, 6)
    )
    kept = jnp.where(lax.bitwise_and(lane, 127) == cell, spread, 0.0).astype(BF16)
    r, c = iota((768, 128), 0), iota((768, 128), 1)
    collect = (lax.shift_right_logical(r, 7) == c).astype(F32).astype(BF16)
    return dot(kept, collect, 1, 0)


def second_gradient(lhs, dout, gb):
    for k in range(9):
        grad = dot(second_rows(lhs, k), dout, 0, 0)
        gb[k * 192 : (k + 1) * 192, :] = grad[64:256].astype(BF16)


def hidden_gradient(dout, wp, back):
    for k in range(9):
        back[k] = dot(dout, wp[k], 1, 1).astype(F32)


def norm_backward(back, cen, gain, rstd, dn):
    scale = gain * rstd
    bottom = iota((8, 8, 128), 1) == 7
    sums = jnp.zeros((1, 128), F32)
    products = jnp.zeros((1, 128), F32)
    for t in range(8):
        planes = []
        for k in range(9):
            part = back[k, t * 64 : (t + 1) * 64, 128:256]
            if t < 7:
                part = part + back[k, (t + 1) * 64 : (t + 2) * 64, 0:128]
            planes.append(part.reshape(8, 8, 128))
        by_kx = []
        for kx in range(3):
            before = jnp.where(bottom, 0.0, pltpu.roll(planes[kx * 3], 7, 1))
            by_kx.append((planes[kx * 3 + 1], planes[kx * 3 + 2] + before))
        parts = []
        for q in range(2):
            moved = jnp.concatenate(
                [by_kx[0][q][1:], jnp.zeros((1, 8, 128), F32)], axis=0
            )
            parts.append((by_kx[1][q], by_kx[2][q] + moved))
        dh = jnp.stack(
            [
                jnp.stack([parts[0][0], parts[1][0]], axis=1),
                jnp.stack([parts[0][1], parts[1][1]], axis=1),
            ],
            axis=1,
        ).reshape(256, 128)
        dh = dh.astype(BF16).astype(F32)
        c = cen[:, lanes(t)]
        n = c * scale
        s = jax.nn.sigmoid(n)
        d = dh * (s * (1.0 + n * (1.0 - s)))
        dn[:, lanes(t)] = d
        sums = sums + jnp.sum(d, axis=0, keepdims=True)
        products = products + jnp.sum(d * c, axis=0, keepdims=True)
    sums = (sums + pltpu.roll(sums, 64, 1)) * (1.0 / 4096.0)
    products = products + pltpu.roll(products, 64, 1)
    slope = products * (rstd * rstd * (1.0 / 4096.0))
    for t in range(8):
        d = dn[:, lanes(t)]
        dn[:, lanes(t)] = scale * (d - sums - cen[:, lanes(t)] * slope)
    return products * rstd


def first_gradient(sel, mx, dn, gs):
    right = dn[...].astype(BF16)
    row = iota((128, 128), 0)
    z = lax.bitwise_and(row, 31)
    upper = (iota((128, 128), 1) >= 64).astype(jnp.int32)
    for kx in range(3):
        for i in range(3):
            full = dot(first_rows(mx, kx, i), right, 0, 0)
            for kz in range(3):
                total = jnp.zeros((128, 128), F32)
                for t in range(8):
                    tap = z - 2 * (2 * t + upper) + 1
                    total = total + jnp.where(tap == kz, full[:, lanes(t)], 0.0)
                total = jnp.sum(total.reshape(4, 32, 128), axis=1)
                total = total + pltpu.roll(total, 64, 1)
                for ky in range(3):
                    value = jnp.zeros((1, 128), F32)
                    for g in range(4):
                        value = jnp.where(
                            lax.rem(sel + ky, 4) == g, total[g : g + 1], value
                        )
                    at = ((kx * 3 + ky) * 3 + kz) * 3 + i
                    gs[at : at + 1, :] = value


def cell_masks(coords):
    _, by, bz = coords
    y, z = iota((40, 256), 0), iota((40, 256), 1)
    in_y = (y < 32) | ((y < 34) & (by < 3)) | ((y >= 38) & (by > 0))
    in_z = (z < 128) | ((z < 130) & (bz < 7)) | ((z >= 254) & (bz > 0))
    return jnp.where(in_y & in_z, 1.0 / 6.0, 0.0).astype(F32)


def divergence(vel_ref, rim_x, rim_y, rim_z, flags, window):
    first_row = iota((32, 128), 0) == 0
    first_lane = iota((32, 128), 1) == 0

    def layer(x, before):
        ux, uy, uz = vel_ref[0, 0, x], vel_ref[0, 1, x], vel_ref[0, 2, x]
        y_rim = rim_y[x : x + 1, :] * flags[2]
        y_before = jnp.where(first_row, y_rim, pltpu.roll(uy, 1, 0))
        z_rim = pltpu.roll(rim_z[...], (128 - x) % 128, 1) * flags[4]
        z_before = jnp.where(first_lane, z_rim, pltpu.roll(uz, 1, 1))
        total = (ux - before) + (uy - y_before) + (uz - z_before)
        window[x + 2, 0:32, 0:128] = -total

    layer(0, rim_x[...] * flags[0])

    for x in range(1, 32):
        layer(x, vel_ref[0, 0, x - 1])


def pack_rim_z(vel_ref, send):
    lane = iota((32, 128), 1)
    packed = jnp.zeros((32, 128), F32)
    for x in range(32):
        moved = pltpu.roll(vel_ref[0, 2, x], (x + 1) % 128, 1)
        packed = jnp.where(lane == x, moved, packed)
    send[...] = packed


def pack_y(field, h, send):
    for r in range(h):
        send[0, r] = field[h : h + 32, 32 - h + r, 0:128]
        send[1, r] = field[h : h + 32, r, 0:128]


def unpack_xy(field, h, got, edges, flags):
    if flags is not None:
        field[0:h, 0:32, 0:128] = field[0:h, 0:32, 0:128] * flags[0]
        field[h + 32 :, 0:32, 0:128] = field[h + 32 :, 0:32, 0:128] * flags[1]
    else:
        flags = [1.0] * 6
    for side, at in ((0, 40 - h), (1, 32)):
        for r in range(h):
            row = at + r
            field[h : h + 32, row, 0:128] = got[side, r] * flags[2 + side]
            for end, low, take in ((0, 0, 8 - h), (1, h + 32, 0)):
                both = flags[2 + side] * flags[end]
                strip = edges[end * 2 + side, r] * both
                for k in range(h):
                    field[low + k, row : row + 1, 0:128] = strip[take + k : take + k + 1]


def pack_z(field, count, h, send):
    lane = iota((40, 128), 1)
    high = jnp.zeros((40, 128), F32)
    low = jnp.zeros((40, 128), F32)
    for x in range(count):
        here = (lane >= x * h) & (lane < x * h + h)
        own = field[x, :, 0:128]
        high = jnp.where(here, pltpu.roll(own, (x * h + h) % 128, 1), high)
        low = jnp.where(here, pltpu.roll(own, x * h, 1) if x else own, low)
    send[0] = high
    send[1] = low


def unpack_z(field, count, h, got, flags):
    lane = iota((40, 128), 1)
    below, above = got[0] * flags[4], got[1] * flags[5]
    for x in range(count):
        lower = pltpu.roll(below, (128 - h - x * h) % 128, 1)
        upper = pltpu.roll(above, (-x * h) % 128, 1) if x else above
        field[x, :, 128:256] = jnp.where(
            lane < h, upper, jnp.where(lane >= 128 - h, lower, 0.0)
        )


def neighbours(field, at):
    own = field[at]
    across = field[at - 1] + field[at + 1]
    along = pltpu.roll(own, 1, 0) + pltpu.roll(own, 39, 0)
    return own, across + along + pltpu.roll(own, 1, 1) + pltpu.roll(own, 255, 1)


def local_solve(window, mask, za, zb, flags, pressure, emit):
    def inside(xi):
        if isinstance(xi, int):
            return flags[0] if xi < 2 else flags[1] if xi > 33 else 1.0
        return jnp.where(xi < 2, flags[0], jnp.where(xi > 33, flags[1], 1.0))

    for z in (za, zb):
        z[0] = jnp.zeros((40, 256), F32)
        z[37] = jnp.zeros((40, 256), F32)

    def first(xi):
        w = window[xi]
        if pressure is not None:
            own, around = neighbours(pressure, xi + 1)
            w = w - (6.0 * own - around)
            window[xi] = w
        za[xi + 1] = w * (mask[...] * inside(xi))

    def sweep(source, target):
        def step(xi):
            _, around = neighbours(source, xi + 1)
            target[xi + 1] = (window[xi] + around) * (mask[...] * inside(xi))

        return step

    def last(xi):
        _, around = neighbours(za, xi + 1)
        z = (window[xi] + around) * mask[...]
        emit(xi, z[0:32, 0:128])

    def over(low, high, body):
        half = (high - low) // 2

        def both(m, carry):
            for k in range(half):
                body(low + m * half + k)
            return carry

        lax.fori_loop(0, 2, both, 0)

    over(0, 36, first)
    over(0, 36, sweep(za, zb))
    over(1, 35, sweep(zb, za))
    over(2, 34, last)


SCRATCH = dict(
    wg=((36, 8, 128), F32),
    table=((36, 32, 1024), BF16),
    mx=((3, 17, 2, 16, 128), BF16),
    cen=((256, 1024), F32),
    lhs=((9, 64, 1152), BF16),
    wp=((9, 256, 128), BF16),
    hp=((128, 128), BF16),
    back=((9, 512, 256), F32),
    dn=((256, 1024), F32),
    wide=((8, 768), F32),
    rows=((32, 128), F32),
    t0=((32, 128), BF16),
    t1=((RANKS, 32, 128), BF16),
    stage=((RANKS, 32, 128), BF16),
    t2=((RANKS, 32, 128), BF16),
    gb=((RANKS * BIG, 128), BF16),
    r1=((RANKS, BIG, 128), BF16),
    part=((RANKS, 8, 128), F32),
    r2=((RANKS, 8, 128), F32),
    whole=((RANKS, 8, 128), F32),
    gathered=((RANKS, BIG, 128), BF16),
    gs=((RANKS * SMALL, 128), F32),
    r1s=((RANKS, SMALL, 128), F32),
    r2s=((RANKS, SMALL, 128), F32),
    gathered_s=((RANKS, SMALL, 128), F32),
    rim_x=((32, 128), F32),
    rim_y=((32, 128), F32),
    rim_z=((32, 128), F32),
    rim_ys=((32, 128), F32),
    rim_zs=((32, 128), F32),
    window=((36, 40, 256), F32),
    press=((38, 40, 256), F32),
    za=((38, 40, 256), F32),
    zb=((38, 40, 256), F32),
    mask=((40, 256), F32),
    wys=((2, 2, 32, 128), F32),
    wyr=((2, 2, 32, 128), F32),
    wer=((4, 2, 8, 128), F32),
    wzs=((2, 40, 128), F32),
    wzr=((2, 40, 128), F32),
    pys=((2, 3, 32, 128), F32),
    pyr=((2, 3, 32, 128), F32),
    per=((4, 3, 8, 128), F32),
    pzs=((2, 40, 128), F32),
    pzr=((2, 40, 128), F32),
)
STEPS = ("t1", "t2", "g1", "g2", "g3", "g4", "s1", "s2", "s3", "rim", "wxy", "wz", "pxy", "pz")


def kernel(*refs):
    (sel_ref, asg_ref, vel_ref, w1_ref, gain_ref, w2_ref, head_ref, target_ref) = refs[:8]
    pressure_ref, pred_ref, grad_ref, small_ref = refs[8:12]
    s = dict(zip(SCRATCH, refs[12 : 12 + len(SCRATCH)]))
    send_sem, recv_sem = refs[12 + len(SCRATCH) :]

    me = lax.axis_index("sec") * 128 + lax.axis_index("dom")
    a, b = lax.div(me, 16), lax.rem(me, 16)
    coords = (lax.div(me, 32), lax.rem(lax.div(me, 8), 4), lax.rem(me, 8))
    bx, by, bz = coords
    flags = [
        jnp.where(cond, 1.0, 0.0).astype(F32)
        for cond in (bx > 0, bx < 7, by > 0, by < 3, bz > 0, bz < 7)
    ]

    def device(f):
        return (lax.div(f, 128), lax.rem(f, 128))

    def box(x, y, z):
        return device(
            lax.rem(bx + x + 8, 8) * 32 + lax.rem(by + y + 4, 4) * 8 + lax.rem(bz + z + 8, 8)
        )

    above = [box(1, 0, 0), box(0, 1, 0), box(0, 0, 1)]
    below = [box(-1, 0, 0), box(0, -1, 0), box(0, 0, -1)]
    corners = [box(1, 1, 0), box(1, -1, 0), box(-1, 1, 0), box(-1, -1, 0)]
    a_ranks = [None] + [lax.rem(a + j, RANKS) for j in range(1, RANKS)]
    b_ranks = [None] + [lax.rem(b + j, RANKS) for j in range(1, RANKS)]
    a_peers = [None] + [device(a_ranks[j] * 16 + b) for j in range(1, RANKS)]
    b_peers = [None] + [device(a * 16 + b_ranks[j]) for j in range(1, RANKS)]

    barrier = pltpu.get_barrier_semaphore()
    everyone = a_peers[1:] + b_peers[1:] + above + below + corners
    for other in everyone:
        pl.semaphore_signal(barrier, inc=1, device_id=other, device_id_type=MESH)

    started = []
    flights = {}

    def start(step, at, source, target, other):
        index = STEPS.index(step) * 16 + at
        copy = pltpu.make_async_remote_copy(
            src_ref=source,
            dst_ref=target,
            send_sem=send_sem.at[index],
            recv_sem=recv_sem.at[index],
            device_id=other,
            device_id_type=MESH,
        )
        copy.start()
        started.append(copy)
        flights.setdefault(step, []).append(copy)

    def arrive(step, sent=False):
        for copy in flights[step]:
            copy.wait_recv()
            if sent:
                copy.wait_send()
                started[:] = [other for other in started if other is not copy]

    def start_xy(step, field, h, send, got, edges):
        low, high = slice(0, 32), slice(0, 128)
        start(step, 0, field.at[32 : 32 + h, low, high], field.at[0:h, low, high], above[0])
        start(
            step, 1, field.at[h : 2 * h, low, high], field.at[32 + h : 32 + 2 * h, low, high], below[0]
        )
        pack_y(field, h, send)
        start(step, 2, send.at[0], got.at[0], above[1])
        start(step, 3, send.at[1], got.at[1], below[1])
        for k, (side, at) in enumerate(((0, 24), (1, 24), (0, 0), (1, 0))):
            start(step, 4 + k, send.at[side, :, at : at + 8, :], edges.at[k], corners[k])

    def start_z(step, send, got):
        start(step, 0, send.at[0], got.at[0], above[2])
        start(step, 1, send.at[1], got.at[1], below[2])

    sel = sel_ref[0, 0]
    window, press = s["window"], s["press"]
    flat = target_ref[0].astype(F32)
    s["rows"][...] = jnp.zeros((32, 128), F32)
    for r in range(24):
        s["rows"][r : r + 1, :] = flat[:, lanes(r)]
    s["t0"][...] = s["rows"][...].astype(BF16)
    s["t1"][a] = s["t0"][...]
    pack_rim_z(vel_ref, s["rim_zs"])
    s["rim_ys"][...] = vel_ref[0, 1, :, 31, :]
    build_first_weights(sel, w1_ref, s["wg"], s["table"])

    pl.semaphore_wait(barrier, len(everyone))

    for j in range(1, RANKS):
        start("t1", j, s["t0"], s["t1"].at[a], a_peers[j])
    start("rim", 0, vel_ref.at[0, 0, 31], s["rim_x"], above[0])
    start("rim", 1, s["rim_ys"], s["rim_y"], above[1])
    start("rim", 2, s["rim_zs"], s["rim_z"], above[2])

    build_rows(sel, vel_ref, s["mx"])
    first_layer(s["mx"], s["table"], s["cen"])
    s["mask"][...] = cell_masks(coords)
    window[:, 32:40, 0:128] = jnp.zeros((36, 8, 128), F32)
    press[:, 32:40, 0:128] = jnp.zeros((38, 8, 128), F32)
    s["hp"][...] = jnp.zeros((128, 128), BF16)
    s["hp"][0:6, :] = head_ref[...]
    build_second_weights(w2_ref, s["wp"])

    arrive("t1")
    for q in range(RANKS):
        s["stage"][q] = s["t1"][lax.div(asg_ref[a * 16 + q], 16)]
    for j in range(1, RANKS):
        start("t2", j, s["stage"].at[b_ranks[j]], s["t2"].at[b], b_peers[j])
    s["t2"][b] = s["stage"][b]
    arrive("rim")
    divergence(vel_ref, s["rim_x"], s["rim_y"], s["rim_z"], flags, window)
    start_xy("wxy", window, 2, s["wys"], s["wyr"], s["wer"])

    gain, rstd = normalise(s["cen"], gain_ref)
    hidden_rows(s["cen"], gain * rstd, s["lhs"])
    out = second_layer(s["lhs"], s["wp"])
    sig = jax.nn.sigmoid(out)
    deep = (out * sig).astype(BF16)
    slope = sig * (1.0 + out * (1.0 - sig))
    stress = dot(deep, s["hp"][...], 1, 1)
    pred_ref[...] = dot(stress.astype(BF16), cell_order(), 0, 0)[0:8]

    arrive("wxy", True)
    unpack_xy(window, 2, s["wyr"], s["wer"], None)
    pack_z(window, 36, 2, s["wzs"])
    start_z("wz", s["wzs"], s["wzr"])

    arrive("t2")
    target = s["t2"][lax.rem(asg_ref[me], 16)].astype(F32)
    error = (stress - target_rows(target, s["wide"])).astype(BF16)
    dout = dot(error, s["hp"][...], 1, 0).astype(BF16).astype(F32) * slope
    dout = dout.astype(BF16)
    s["gb"][1728:1792, :] = jnp.zeros((64, 128), BF16)
    second_gradient(s["lhs"], dout, s["gb"])
    for j in range(1, RANKS):
        rows = pl.ds(pl.multiple_of(a_ranks[j] * BIG, 16), BIG)
        start("g1", j, s["gb"].at[rows], s["r1"].at[j], a_peers[j])

    arrive("wz")
    unpack_z(window, 36, 2, s["wzr"], flags)

    def keep(xi, z):
        press[xi + 1, 0:32, 0:128] = z

    local_solve(window, s["mask"], s["za"], s["zb"], flags, None, keep)
    start_xy("pxy", press, 3, s["pys"], s["pyr"], s["per"])

    gs = s["gs"]
    gs[...] = jnp.zeros((128, 128), F32)
    gs[82:88, :] = dot(error, deep, 0, 0)[0:6]
    hidden_gradient(dout, s["wp"], s["back"])
    gs[81:82, :] = norm_backward(s["back"], s["cen"], gain, rstd, s["dn"])
    first_gradient(sel, s["mx"], s["dn"], gs)
    for j in range(1, RANKS):
        rows = pl.ds(pl.multiple_of(a_ranks[j] * SMALL, 8), SMALL)
        start("s1", j, gs.at[rows], s["r1s"].at[j], a_peers[j])

    arrive("g1")
    big = s["gb"][pl.ds(pl.multiple_of(a * BIG, 16), BIG), :].astype(F32)
    for j in range(1, RANKS):
        big = big + s["r1"][j].astype(F32)
    part = s["part"]
    part[0:14] = big.reshape(14, 8, 128)
    part[14:16] = jnp.zeros((2, 8, 128), F32)
    for j in range(1, RANKS):
        start("g2", j, part.at[b_ranks[j]], s["r2"].at[j], b_peers[j])

    arrive("pxy", True)
    unpack_xy(press, 3, s["pyr"], s["per"], flags)
    pack_z(press, 38, 3, s["pzs"])
    start_z("pz", s["pzs"], s["pzr"])

    arrive("s1")
    small = gs[pl.ds(pl.multiple_of(a * SMALL, 8), SMALL), :]
    for j in range(1, RANKS):
        small = small + s["r1s"][j]
    s["r2s"][b] = small
    for j in range(1, RANKS):
        start("s2", j, s["r2s"].at[b], s["r2s"].at[b], b_peers[j])

    arrive("g2")
    total = part[b]
    for j in range(1, RANKS):
        total = total + s["r2"][j]
    s["whole"][b] = total
    for j in range(1, RANKS):
        start("g3", j, s["whole"].at[b], s["whole"].at[b], b_peers[j])

    arrive("pz")
    unpack_z(press, 38, 3, s["pzr"], flags)

    def finish(xi, z):
        pressure_ref[xi - 2] = press[xi + 1, 0:32, 0:128] + z

    local_solve(window, s["mask"], s["za"], s["zb"], flags, press, finish)

    arrive("s2")
    small = s["r2s"][0]
    for q in range(1, RANKS):
        small = small + s["r2s"][q]
    s["gathered_s"][a] = small
    for j in range(1, RANKS):
        start("s3", j, s["gathered_s"].at[a], s["gathered_s"].at[a], a_peers[j])

    arrive("g3")
    gathered = s["gathered"]
    gathered[a] = s["whole"][0:14].reshape(BIG, 128).astype(BF16)
    for j in range(1, RANKS):
        start("g4", j, gathered.at[a], gathered.at[a], a_peers[j])
    arrive("s3")
    small_ref[...] = s["gathered_s"][...].reshape(RANKS * SMALL, 128)
    arrive("g4")
    grad_ref[...] = gathered[...]
    for copy in started:
        copy.wait_send()


def finish_kernel(
    pressure_in, pred_in, grad_in, small_in, pressure_out, pred_out, first, gain, second, head
):
    pressure_out[0] = pressure_in[...]
    for k in range(6):
        pred_out[0, :, lanes(k, 512)] = pred_in[k : k + 1, :].astype(BF16)
    flat = grad_in[...].reshape(RANKS * BIG, 128)
    for kx in range(3):
        for ky in range(3):
            for kz in range(3):
                k = (kx * 3 + ky) * 3 + kz
                second[kx, ky, kz] = flat[k * 64 : (k + 1) * 64].astype(F32)
                first[kx, ky, kz] = small_in[k * 3 : k * 3 + 3, 0:64]
    gain[...] = small_in[81:82, 0:64]
    head[...] = small_in[82:88, :]


def shards(
    velocity,
    first_kernel,
    norm_gain,
    second_kernel,
    head_weight,
    selection,
    assignment,
    target_stress,
):
    vmem = pl.BlockSpec(memory_space=pltpu.VMEM)
    smem = pl.BlockSpec(memory_space=pltpu.SMEM)
    semaphores = 16 * len(STEPS)
    pressure, stress, grads, small = pl.pallas_call(
        kernel,
        out_shape=[
            jax.ShapeDtypeStruct((32, 32, 128), F32),
            jax.ShapeDtypeStruct((8, 512), F32),
            jax.ShapeDtypeStruct((RANKS, BIG, 128), BF16),
            jax.ShapeDtypeStruct((RANKS * SMALL, 128), F32),
        ],
        in_specs=[smem, smem] + [vmem] * 6,
        out_specs=[vmem] * 4,
        scratch_shapes=[pltpu.VMEM(shape, kind) for shape, kind in SCRATCH.values()]
        + [pltpu.SemaphoreType.DMA((semaphores,))] * 2,
        compiler_params=pltpu.CompilerParams(
            collective_id=0, has_side_effects=True, vmem_limit_bytes=56 << 20
        ),
    )(
        selection,
        assignment.reshape(-1),
        velocity,
        first_kernel,
        norm_gain.reshape(1, 64),
        second_kernel,
        head_weight.T,
        target_stress,
    )
    pressure, predicted, first, gain, second, head = pl.pallas_call(
        finish_kernel,
        out_shape=[
            jax.ShapeDtypeStruct((1, 32, 32, 128), F32),
            jax.ShapeDtypeStruct((1, 1, 3072), BF16),
            jax.ShapeDtypeStruct((3, 3, 3, 3, 64), F32),
            jax.ShapeDtypeStruct((1, 64), F32),
            jax.ShapeDtypeStruct((3, 3, 3, 64, 128), F32),
            jax.ShapeDtypeStruct((6, 128), F32),
        ],
        in_specs=[vmem] * 4,
        out_specs=[vmem] * 6,
    )(pressure, stress, grads, small)
    return (pressure, predicted, first, gain.reshape(64), second, head.T)


def solution(mesh):
    placed = (
        P(("sec", "dom"), None, None, None, None),
        P(),
        P(),
        P(),
        P(),
        P(("sec", "dom"), None),
        P(),
        P(("sec", "dom"), None, None),
    )
    return jax.shard_map(
        shards,
        mesh=mesh,
        in_specs=placed,
        out_specs=(
            P(("sec", "dom"), None, None, None),
            P(("sec", "dom"), None, None),
            P(),
            P(),
            P(),
            P(),
        ),
        check_vma=False,
    )
```

```python
import jax
import jax.numpy as jnp
from jax import lax
from jax.experimental import pallas as pl
from jax.experimental.pallas import tpu as pltpu
from jax.sharding import PartitionSpec as P

F32 = jnp.float32
BF16 = jnp.bfloat16
NORM_EPS = 1e-05
MESH = pl.DeviceIdType.MESH
RANKS = 16
OWNERS = 32
TAPS = 27
BIG = 64
SMALL = 8


def iota(shape, dim):
    return lax.broadcasted_iota(jnp.int32, shape, dim)


def dot(left, right, cl, cr):
    return lax.dot_general(
        left, right, (((cl,), (cr,)), ((), ())), preferred_element_type=F32
    )


def lanes(t, width=128):
    return slice(t * width, (t + 1) * width)


def build_first_weights(sel, w1_ref, wg, table):
    for kx in range(3):
        for kz in range(3):
            rows = []
            for ky in range(3):
                w = w1_ref[kx, ky, kz].astype(F32)
                rows.append(jnp.concatenate([w, w], axis=1))
            for g in range(4):
                mixed = jnp.zeros((3, 128), F32)
                for ky in range(3):
                    mixed = jnp.where(lax.rem(sel + ky, 4) == g, rows[ky], mixed)
                for i in range(3):
                    wg[(kx * 3 + i) * 4 + g, kz : kz + 1, :] = mixed[i : i + 1]
    row = iota((32, 128), 0)
    upper = (iota((32, 128), 1) >= 64).astype(jnp.int32)
    for t in range(8):
        tap = row - 2 * (2 * t + upper) + 1
        masks = [(tap == k).astype(F32) for k in range(3)]

        for c in range(0, 36, 12):
            w = wg[c : c + 12]
            block = sum(masks[k][None] * w[:, k : k + 1, :] for k in range(3))
            table[c : c + 12, :, lanes(t)] = block.astype(BF16)


def build_rows(sel, vel_ref, mx):
    keep = lax.shift_right_logical(iota((8, 8, 128), 2), 5) == sel
    top = iota((8, 8, 128), 1) == 0
    for i in range(3):
        mx[i, 0, 0] = jnp.zeros((16, 128), BF16)
        for m in range(0, 16, 4):
            d = []
            for o in range(4):
                rows = vel_ref[i, 2 * m : 2 * m + 8, pl.ds(o, 8, stride=4), :]
                d.append(jnp.where(keep, rows, 0.0))
            before = jnp.where(top, 0.0, pltpu.roll(d[3], 1, 1))
            even = before + pltpu.roll(d[0], 32, 2) + pltpu.roll(d[1], 64, 2)
            odd = d[1] + pltpu.roll(d[2], 32, 2) + pltpu.roll(d[3], 64, 2)
            both = jnp.concatenate([even, odd], axis=1).astype(BF16)
            both = both.reshape(4, 2, 16, 128)
            mx[i, m : m + 4, 1] = both[:, 0]
            mx[i, m + 1 : m + 5, 0] = both[:, 1]


def first_rows(mx, kx, i):
    if kx == 0:
        part = mx[i, 0:16, 0]
    elif kx == 1:
        part = mx[i, 0:16, 1]
    else:
        part = mx[i, 1:17, 0]
    return part.reshape(256, 128)


def fold_channels(row):
    total = row[:, lanes(0)]
    for t in range(1, 8):
        total = total + row[:, lanes(t)]
    return total + pltpu.roll(total, 64, 1)


def first_layer(mx, table, cen):
    left = jnp.concatenate(
        [first_rows(mx, kx, i) for kx in range(3) for i in range(3)], axis=1
    )
    for t in range(4):
        right = table[:, :, lanes(t, 256)].reshape(1152, 256)
        cen[:, lanes(t, 256)] = dot(left, right, 1, 0)


def normalise(cen, gain_ref):
    total = fold_channels(jnp.sum(cen[...], axis=0, keepdims=True))
    mean = total * (1.0 / 4096.0)
    square = jnp.zeros((1, 128), F32)
    for t in range(8):
        c = cen[:, lanes(t)] - mean
        cen[:, lanes(t)] = c
        square = square + jnp.sum(c * c, axis=0, keepdims=True)
    var = (square + pltpu.roll(square, 64, 1)) * (1.0 / 4096.0)
    gain = gain_ref[0:1, :]
    gain = jnp.concatenate([gain, gain], axis=1)
    return gain, lax.rsqrt(var + NORM_EPS)


def hidden_rows(cen, scale, lhs):
    top = iota((16, 8, 128), 1) == 0
    for k in range(9):
        lhs[k, :, 0:128] = jnp.zeros((64, 128), BF16)
    for t in range(8):
        n = cen[:, lanes(t)] * scale
        h = (n * jax.nn.sigmoid(n)).reshape(16, 2, 8, 128)
        even, odd = h[:, 0], h[:, 1]
        before = jnp.where(top, 0.0, pltpu.roll(odd, 1, 1))
        for ky, plane in ((0, before), (1, even), (2, odd)):
            plane = plane.reshape(8, 2, 8, 128)
            low, high = plane[:, 0], plane[:, 1]
            shifted = jnp.concatenate([jnp.zeros((1, 8, 128), F32), high[:7]], axis=0)
            for kx, part in ((0, shifted), (1, low), (2, high)):
                lhs[kx * 3 + ky, :, lanes(t + 1)] = part.reshape(64, 128).astype(BF16)


def second_rows(lhs, k):
    return jnp.concatenate(
        [lhs[k, :, p * 128 : p * 128 + 256] for p in range(8)], axis=0
    )


def second_layer(lhs, wp):
    out = jnp.zeros((512, 128), F32)
    for k in range(9):
        out = out + dot(second_rows(lhs, k), wp[k // 3, k % 3].reshape(256, 128), 1, 0)
    return out


def cell_order():
    r, c = iota((512, 512), 0), iota((512, 512), 1)
    same = (lax.shift_right_logical(c, 3) == lax.bitwise_and(r, 63)) & (
        lax.bitwise_and(c, 7) == lax.shift_right_logical(r, 6)
    )
    return same.astype(F32).astype(BF16)


def target_rows(flat, wide):
    wide[...] = jnp.zeros((8, 768), F32)
    for k in range(6):
        wide[0:4, lanes(k)] = flat[4 * k : 4 * k + 4]
    row = iota((512, 8), 0)
    which = lax.bitwise_and(lax.shift_right_logical(row, 4), 3)
    pick = (which == iota((512, 8), 1)).astype(F32).astype(BF16)
    spread = dot(pick, wide[...].astype(BF16), 1, 0)
    row, lane = iota((512, 768), 0), iota((512, 768), 1)
    cell = (
        lax.bitwise_and(lax.shift_right_logical(row, 3), 1) * 64
        + lax.bitwise_and(row, 7) * 8
        + lax.shift_right_logical(row, 6)
    )
    kept = jnp.where(lax.bitwise_and(lane, 127) == cell, spread, 0.0).astype(BF16)
    r, c = iota((768, 128), 0), iota((768, 128), 1)
    collect = (lax.shift_right_logical(r, 7) == c).astype(F32).astype(BF16)
    return dot(kept, collect, 1, 0)


def second_gradient(lhs, dout, gb):
    for k in range(9):
        grad = dot(second_rows(lhs, k), dout, 0, 0)
        gb[k * 192 : (k + 1) * 192, :] = grad[64:256].astype(BF16)


def hidden_gradient(dout, wp, back):
    for k in range(9):
        back[k] = dot(dout, wp[k // 3, k % 3].reshape(256, 128), 1, 1)


def norm_backward(back, cen, gain, rstd, dn):
    scale = gain * rstd
    bottom = iota((8, 8, 128), 1) == 7
    sums = jnp.zeros((1, 128), F32)
    products = jnp.zeros((1, 128), F32)
    for t in range(8):
        planes = []
        for k in range(9):
            part = back[k, t * 64 : (t + 1) * 64, 128:256]
            if t < 7:
                part = part + back[k, (t + 1) * 64 : (t + 2) * 64, 0:128]
            planes.append(part.reshape(8, 8, 128))
        by_kx = []
        for kx in range(3):
            before = jnp.where(bottom, 0.0, pltpu.roll(planes[kx * 3], 7, 1))
            by_kx.append((planes[kx * 3 + 1], planes[kx * 3 + 2] + before))
        parts = []
        for q in range(2):
            moved = jnp.concatenate(
                [by_kx[0][q][1:], jnp.zeros((1, 8, 128), F32)], axis=0
            )
            parts.append((by_kx[1][q], by_kx[2][q] + moved))
        dh = jnp.stack(
            [
                jnp.stack([parts[0][0], parts[1][0]], axis=1),
                jnp.stack([parts[0][1], parts[1][1]], axis=1),
            ],
            axis=1,
        ).reshape(256, 128)
        dh = dh.astype(BF16).astype(F32)
        c = cen[:, lanes(t)]
        n = c * scale
        s = jax.nn.sigmoid(n)
        d = dh * (s * (1.0 + n * (1.0 - s)))
        dn[:, lanes(t)] = d
        sums = sums + jnp.sum(d, axis=0, keepdims=True)
        products = products + jnp.sum(d * c, axis=0, keepdims=True)
    sums = (sums + pltpu.roll(sums, 64, 1)) * (1.0 / 4096.0)
    products = products + pltpu.roll(products, 64, 1)
    slope = products * (rstd * rstd * (1.0 / 4096.0))
    for t in range(8):
        d = dn[:, lanes(t)]
        dn[:, lanes(t)] = scale * (d - sums - cen[:, lanes(t)] * slope)
    return products * rstd


def first_gradient(sel, mx, dn, gs):
    right = dn[...].astype(BF16)
    row = iota((128, 128), 0)
    z = lax.bitwise_and(row, 31)
    upper = (iota((128, 128), 1) >= 64).astype(jnp.int32)
    for kx in range(3):
        for i in range(3):
            full = dot(first_rows(mx, kx, i), right, 0, 0)
            for kz in range(3):
                total = jnp.zeros((128, 128), F32)
                for t in range(8):
                    tap = z - 2 * (2 * t + upper) + 1
                    total = total + jnp.where(tap == kz, full[:, lanes(t)], 0.0)
                total = jnp.sum(total.reshape(4, 32, 128), axis=1)
                total = total + pltpu.roll(total, 64, 1)
                for ky in range(3):
                    value = jnp.zeros((1, 128), F32)
                    for g in range(4):
                        value = jnp.where(
                            lax.rem(sel + ky, 4) == g, total[g : g + 1], value
                        )
                    at = ((kx * 3 + ky) * 3 + kz) * 3 + i
                    gs[at : at + 1, :] = value


def cell_masks(coords):
    _, by, bz = coords
    y, z = iota((40, 256), 0), iota((40, 256), 1)
    in_y = (y < 32) | ((y < 34) & (by < 3)) | ((y >= 38) & (by > 0))
    in_z = (z < 128) | ((z < 130) & (bz < 7)) | ((z >= 254) & (bz > 0))
    return jnp.where(in_y & in_z, 1.0 / 6.0, 0.0).astype(F32)


def divergence(vel_ref, rim_x, rim_y, rim_z, flags, window):
    first_row = iota((32, 128), 0) == 0
    first_lane = iota((32, 128), 1) == 0

    def layer(x, before):
        ux, uy, uz = vel_ref[0, x], vel_ref[1, x], vel_ref[2, x]
        y_rim = rim_y[x : x + 1, :] * flags[2]
        y_before = jnp.where(first_row, y_rim, pltpu.roll(uy, 1, 0))
        z_rim = pltpu.roll(rim_z[...], (128 - x) % 128, 1) * flags[4]
        z_before = jnp.where(first_lane, z_rim, pltpu.roll(uz, 1, 1))
        total = (ux - before) + (uy - y_before) + (uz - z_before)
        window[x + 2, 0:32, 0:128] = -total

    layer(0, rim_x[...] * flags[0])

    for x in range(1, 32):
        layer(x, vel_ref[0, x - 1])


def pack_rim_z(vel_ref, send):
    lane = iota((32, 128), 1)
    packed = jnp.zeros((32, 128), F32)
    for x in range(32):
        moved = pltpu.roll(vel_ref[2, x], (x + 1) % 128, 1)
        packed = jnp.where(lane == x, moved, packed)
    send[...] = packed


def pack_y(field, h, send):
    for r in range(h):
        send[0, r] = field[h : h + 32, 32 - h + r, 0:128]
        send[1, r] = field[h : h + 32, r, 0:128]


def unpack_xy(field, h, got, edges, flags):
    if flags is not None:
        field[0:h, 0:32, 0:128] = field[0:h, 0:32, 0:128] * flags[0]
        field[h + 32 :, 0:32, 0:128] = field[h + 32 :, 0:32, 0:128] * flags[1]
    else:
        flags = [1.0] * 6
    for side, at in ((0, 40 - h), (1, 32)):
        for r in range(h):
            row = at + r
            field[h : h + 32, row, 0:128] = got[side, r] * flags[2 + side]
            for end, low, take in ((0, 0, 8 - h), (1, h + 32, 0)):
                both = flags[2 + side] * flags[end]
                strip = edges[end * 2 + side, r] * both
                for k in range(h):
                    field[low + k, row : row + 1, 0:128] = strip[take + k : take + k + 1]


def pack_z(field, count, h, send):
    lane = iota((40, 128), 1)
    high = jnp.zeros((40, 128), F32)
    low = jnp.zeros((40, 128), F32)
    for x in range(count):
        here = (lane >= x * h) & (lane < x * h + h)
        own = field[x, :, 0:128]
        high = jnp.where(here, pltpu.roll(own, (x * h + h) % 128, 1), high)
        low = jnp.where(here, pltpu.roll(own, x * h, 1) if x else own, low)
    send[0] = high
    send[1] = low


def unpack_z(field, count, h, got, flags):
    lane = iota((40, 128), 1)
    below, above = got[0] * flags[4], got[1] * flags[5]
    for x in range(count):
        lower = pltpu.roll(below, (128 - h - x * h) % 128, 1)
        upper = pltpu.roll(above, (-x * h) % 128, 1) if x else above
        field[x, :, 128:256] = jnp.where(
            lane < h, upper, jnp.where(lane >= 128 - h, lower, 0.0)
        )


def neighbours(field, at):
    own = field[at]
    across = field[at - 1] + field[at + 1]
    along = pltpu.roll(own, 1, 0) + pltpu.roll(own, 39, 0)
    return own, across + along + pltpu.roll(own, 1, 1) + pltpu.roll(own, 255, 1)


def local_solve(window, mask, za, zb, flags, pressure, emit):
    def inside(xi):
        if isinstance(xi, int):
            return flags[0] if xi < 2 else flags[1] if xi > 33 else 1.0
        return jnp.where(xi < 2, flags[0], jnp.where(xi > 33, flags[1], 1.0))

    for z in (za, zb):
        z[0] = jnp.zeros((40, 256), F32)
        z[37] = jnp.zeros((40, 256), F32)

    def first(xi):
        w = window[xi]
        if pressure is not None:
            own, around = neighbours(pressure, xi + 1)
            w = w - (6.0 * own - around)
            window[xi] = w
        za[xi + 1] = w * (mask[...] * inside(xi))

    def sweep(source, target):
        def step(xi):
            _, around = neighbours(source, xi + 1)
            target[xi + 1] = (window[xi] + around) * (mask[...] * inside(xi))

        return step

    def last(xi):
        _, around = neighbours(za, xi + 1)
        z = (window[xi] + around) * mask[...]
        emit(xi, z[0:32, 0:128])

    def over(low, high, body):
        half = (high - low) // 2

        def both(m, carry):
            for k in range(half):
                body(low + m * half + k)
            return carry

        lax.fori_loop(0, 2, both, 0)

    over(0, 36, first)
    over(0, 36, sweep(za, zb))
    over(1, 35, sweep(zb, za))
    over(2, 34, last)


SCRATCH = dict(
    wg=((36, 8, 128), F32),
    table=((36, 32, 1024), BF16),
    mx=((3, 17, 2, 16, 128), BF16),
    cen=((256, 1024), F32),
    lhs=((9, 64, 1152), BF16),
    wp=((3, 3, 4, 64, 128), BF16),
    vel=((3, 32, 32, 128), F32),
    done=((32, 32, 128), F32),
    hp=((128, 128), BF16),
    back=((9, 512, 256), F32),
    dn=((256, 1024), F32),
    wide=((8, 768), F32),
    rows=((32, 128), F32),
    t0=((32, 128), BF16),
    t1=((RANKS, 32, 128), BF16),
    stage=((RANKS, 32, 128), BF16),
    t2=((RANKS, 32, 128), BF16),
    gb=((OWNERS * BIG, 128), BF16),
    r1=((OWNERS, BIG, 128), BF16),
    parts=((8, BIG, 128), BF16),
    gathered=((OWNERS, BIG, 128), BF16),
    gs=((RANKS * SMALL, 128), F32),
    r1s=((RANKS, SMALL, 128), F32),
    r2s=((RANKS, SMALL, 128), F32),
    gathered_s=((RANKS, SMALL, 128), F32),
    rim_x=((32, 128), F32),
    rim_y=((32, 128), F32),
    rim_z=((32, 128), F32),
    rim_ys=((32, 128), F32),
    rim_zs=((32, 128), F32),
    window=((36, 40, 256), F32),
    press=((38, 40, 256), F32),
    za=((38, 40, 256), F32),
    zb=((38, 40, 256), F32),
    mask=((40, 256), F32),
    wys=((2, 2, 32, 128), F32),
    wyr=((2, 2, 32, 128), F32),
    wer=((4, 2, 8, 128), F32),
    wzs=((2, 40, 128), F32),
    wzr=((2, 40, 128), F32),
    pys=((2, 3, 32, 128), F32),
    pyr=((2, 3, 32, 128), F32),
    per=((4, 3, 8, 128), F32),
    pzs=((2, 40, 128), F32),
    pzr=((2, 40, 128), F32),
)
GROUP_STEPS = ("t1", "t2", "g1", "g2", "g3", "s1", "s2", "s3")
HALO_STEPS = ("rim", "wxy", "wz", "pxy", "pz")
SEMAPHORES = len(GROUP_STEPS) + 8 * len(HALO_STEPS)


def kernel(*refs):
    (sel_ref, asg_ref, vel_hbm, w1_ref, gain_ref, w2_hbm, head_ref, target_ref) = refs[:8]
    pressure_ref, pred_ref, grad_ref, small_ref = refs[8:12]
    s = dict(zip(SCRATCH, refs[12 : 12 + len(SCRATCH)]))
    send_sem, recv_sem, local_sem = refs[12 + len(SCRATCH) :]
    vel_ref = s["vel"]
    load_velocity = pltpu.make_async_copy(vel_hbm.at[0], vel_ref, local_sem.at[0])
    load_velocity.start()
    load_second = pltpu.make_async_copy(w2_hbm, s["wp"].at[:, :, 1:4], local_sem.at[1])
    load_second.start()

    me = lax.axis_index("sec") * 128 + lax.axis_index("dom")
    a, b = lax.div(me, 16), lax.rem(me, 16)
    z, core = lax.div(b, 2), lax.rem(b, 2)
    c = a * 2 + core
    coords = (lax.div(me, 32), lax.rem(lax.div(me, 8), 4), lax.rem(me, 8))
    bx, by, bz = coords
    flags = [
        jnp.where(cond, 1.0, 0.0).astype(F32)
        for cond in (bx > 0, bx < 7, by > 0, by < 3, bz > 0, bz < 7)
    ]

    def device(f):
        return (lax.div(f, 128), lax.rem(f, 128))

    def box(x, y, z):
        return device(
            lax.rem(bx + x + 8, 8) * 32 + lax.rem(by + y + 4, 4) * 8 + lax.rem(bz + z + 8, 8)
        )

    above = [box(1, 0, 0), box(0, 1, 0), box(0, 0, 1)]
    below = [box(-1, 0, 0), box(0, -1, 0), box(0, 0, -1)]
    corners = [box(1, 1, 0), box(1, -1, 0), box(-1, 1, 0), box(-1, -1, 0)]
    a_ranks = [None] + [lax.rem(a + j, RANKS) for j in range(1, RANKS)]
    b_ranks = [None] + [lax.rem(b + j, RANKS) for j in range(1, RANKS)]
    a_peers = [None] + [device(a_ranks[j] * 16 + b) for j in range(1, RANKS)]
    b_peers = [None] + [device(a * 16 + b_ranks[j]) for j in range(1, RANKS)]

    c_ranks = [None] + [lax.rem(c + j, OWNERS) for j in range(1, OWNERS)]
    c_peers = [None] + [
        device(lax.div(r, 2) * 16 + z * 2 + lax.rem(r, 2)) for r in c_ranks[1:]
    ]
    z_peers = [None] + [
        device(a * 16 + lax.rem(z + j, 8) * 2 + core) for j in range(1, 8)
    ]

    barrier = pltpu.get_barrier_semaphore()
    everyone = c_peers[1:] + b_peers[1:] + above + below + corners
    for other in everyone:
        pl.semaphore_signal(barrier, inc=1, device_id=other, device_id_type=MESH)

    flights = {}

    def remote(index, source, target, other):
        return pltpu.make_async_remote_copy(
            src_ref=source,
            dst_ref=target,
            send_sem=send_sem.at[index],
            recv_sem=recv_sem.at[index],
            device_id=other,
            device_id_type=MESH,
        )

    def start(step, at, source, target, other):
        index = len(GROUP_STEPS) + 8 * HALO_STEPS.index(step) + at
        copy = remote(index, source, target, other)
        copy.start()
        flights.setdefault(step, []).append(copy)

    def start_group(step, source, target, peers):
        for j in range(1, len(peers)):
            remote(GROUP_STEPS.index(step), source(j), target(j), peers[j]).start()

    def arrive_group(step, slots, peers):
        every = remote(GROUP_STEPS.index(step), slots, slots, peers[1])
        every.wait_recv()
        flights[step] = [every]

    def arrive(step, sent=False):
        for copy in flights[step]:
            copy.wait_recv()
            if sent:
                copy.wait_send()
        if sent:
            del flights[step]

    def start_xy(step, field, h, send, got, edges):
        low, high = slice(0, 32), slice(0, 128)
        start(step, 0, field.at[32 : 32 + h, low, high], field.at[0:h, low, high], above[0])
        start(
            step, 1, field.at[h : 2 * h, low, high], field.at[32 + h : 32 + 2 * h, low, high], below[0]
        )
        pack_y(field, h, send)
        start(step, 2, send.at[0], got.at[0], above[1])
        start(step, 3, send.at[1], got.at[1], below[1])
        for k, (side, at) in enumerate(((0, 24), (1, 24), (0, 0), (1, 0))):
            start(step, 4 + k, send.at[side, :, at : at + 8, :], edges.at[k], corners[k])

    def start_z(step, send, got):
        start(step, 0, send.at[0], got.at[0], above[2])
        start(step, 1, send.at[1], got.at[1], below[2])

    sel = sel_ref[0, 0]
    window, press = s["window"], s["press"]
    flat = target_ref[0].astype(F32)
    s["rows"][...] = jnp.zeros((32, 128), F32)
    for r in range(24):
        s["rows"][r : r + 1, :] = flat[:, lanes(r)]
    s["t0"][...] = s["rows"][...].astype(BF16)
    s["t1"][a] = s["t0"][...]
    load_velocity.wait()
    pack_rim_z(vel_ref, s["rim_zs"])
    s["rim_ys"][...] = vel_ref[1, :, 31, :]

    pl.semaphore_wait(barrier, len(everyone))

    start_group("t1", lambda j: s["t0"], lambda j: s["t1"].at[a], a_peers)
    start("rim", 0, vel_ref.at[0, 31], s["rim_x"], above[0])
    start("rim", 1, s["rim_ys"], s["rim_y"], above[1])
    start("rim", 2, s["rim_zs"], s["rim_z"], above[2])

    build_first_weights(sel, w1_ref, s["wg"], s["table"])
    build_rows(sel, vel_ref, s["mx"])
    s["mask"][...] = cell_masks(coords)
    window[:, 32:40, 0:128] = jnp.zeros((36, 8, 128), F32)
    press[:, 32:40, 0:128] = jnp.zeros((38, 8, 128), F32)
    s["hp"][...] = jnp.zeros((128, 128), BF16)
    s["hp"][0:6, :] = head_ref[...]
    s["wp"][:, :, 0] = jnp.zeros((3, 3, 64, 128), BF16)
    s["gb"][TAPS * BIG :, :] = jnp.zeros(((OWNERS - TAPS) * BIG, 128), BF16)

    arrive_group("t1", s["t1"].at[0:15], a_peers)
    for q in range(RANKS):
        s["stage"][q] = s["t1"][lax.div(asg_ref[a * 16 + q], 16)]
    start_group("t2", lambda j: s["stage"].at[b_ranks[j]], lambda j: s["t2"].at[b], b_peers)
    s["t2"][b] = s["stage"][b]
    arrive("rim")
    divergence(vel_ref, s["rim_x"], s["rim_y"], s["rim_z"], flags, window)
    start_xy("wxy", window, 2, s["wys"], s["wyr"], s["wer"])

    first_layer(s["mx"], s["table"], s["cen"])
    gain, rstd = normalise(s["cen"], gain_ref)
    hidden_rows(s["cen"], gain * rstd, s["lhs"])
    load_second.wait()
    out = second_layer(s["lhs"], s["wp"])
    sig = jax.nn.sigmoid(out)
    deep = (out * sig).astype(BF16)
    slope = sig * (1.0 + out * (1.0 - sig))
    stress = dot(deep, s["hp"][...], 1, 1)

    arrive_group("t2", s["t2"].at[0:15], b_peers)
    target = s["t2"][lax.rem(asg_ref[me], 16)].astype(F32)
    error = (stress - target_rows(target, s["wide"])).astype(BF16)
    dout = dot(error, s["hp"][...], 1, 0).astype(BF16).astype(F32) * slope
    dout = dout.astype(BF16)
    second_gradient(s["lhs"], dout, s["gb"])

    def tap_rows(rank):
        return pl.ds(pl.multiple_of(rank * BIG, BIG), BIG)

    def small_rows(rank):
        return pl.ds(pl.multiple_of(rank * SMALL, SMALL), SMALL)

    start_group(
        "g1", lambda j: s["gb"].at[tap_rows(c_ranks[j])], lambda j: s["r1"].at[j], c_peers
    )

    arrive("wxy", True)
    unpack_xy(window, 2, s["wyr"], s["wer"], None)
    pack_z(window, 36, 2, s["wzs"])
    start_z("wz", s["wzs"], s["wzr"])

    gs = s["gs"]
    gs[...] = jnp.zeros((128, 128), F32)
    gs[82:88, :] = dot(error, deep, 0, 0)[0:6]
    hidden_gradient(dout, s["wp"], s["back"])
    gs[81:82, :] = norm_backward(s["back"], s["cen"], gain, rstd, s["dn"])
    first_gradient(sel, s["mx"], s["dn"], gs)
    start_group("s1", lambda j: gs.at[small_rows(a_ranks[j])], lambda j: s["r1s"].at[j], a_peers)

    arrive("wz")
    unpack_z(window, 36, 2, s["wzr"], flags)

    def keep(xi, z):
        press[xi + 1, 0:32, 0:128] = z

    local_solve(window, s["mask"], s["za"], s["zb"], flags, None, keep)
    start_xy("pxy", press, 3, s["pys"], s["pyr"], s["per"])

    arrive_group("g1", s["r1"].at[1:OWNERS], c_peers)
    total = s["gb"][tap_rows(c), :].astype(F32)
    for j in range(1, OWNERS):
        total = total + s["r1"][j].astype(F32)
    s["parts"][z] = total.astype(BF16)
    start_group("g2", lambda j: s["parts"].at[z], lambda j: s["parts"].at[z], z_peers)

    arrive_group("s1", s["r1s"].at[1:RANKS], a_peers)
    small = gs[small_rows(a), :]
    for j in range(1, RANKS):
        small = small + s["r1s"][j]
    s["r2s"][b] = small
    start_group("s2", lambda j: s["r2s"].at[b], lambda j: s["r2s"].at[b], b_peers)
    pred_ref[...] = dot(stress.astype(BF16), cell_order(), 0, 0)[0:8]

    arrive_group("g2", s["parts"].at[0:7], z_peers)
    total = s["parts"][0].astype(F32)
    for q in range(1, 8):
        total = total + s["parts"][q].astype(F32)
    gathered = s["gathered"]
    gathered[c] = total.astype(BF16)
    start_group("g3", lambda j: gathered.at[c], lambda j: gathered.at[c], c_peers)

    arrive("pxy", True)
    unpack_xy(press, 3, s["pyr"], s["per"], flags)
    pack_z(press, 38, 3, s["pzs"])
    start_z("pz", s["pzs"], s["pzr"])

    arrive_group("s2", s["r2s"].at[0:15], b_peers)
    small = s["r2s"][0]
    for q in range(1, RANKS):
        small = small + s["r2s"][q]
    s["gathered_s"][a] = small
    start_group("s3", lambda j: s["gathered_s"].at[a], lambda j: s["gathered_s"].at[a], a_peers)

    arrive("pz")
    unpack_z(press, 38, 3, s["pzr"], flags)

    def finish(xi, z):
        s["done"][xi - 2] = press[xi + 1, 0:32, 0:128] + z

    local_solve(window, s["mask"], s["za"], s["zb"], flags, press, finish)
    store_pressure = pltpu.make_async_copy(s["done"], pressure_ref, local_sem.at[2])
    store_pressure.start()

    arrive_group("g3", gathered.at[0 : OWNERS - 1], c_peers)
    store_gradient = pltpu.make_async_copy(gathered.at[0:TAPS], grad_ref, local_sem.at[3])
    store_gradient.start()
    arrive_group("s3", s["gathered_s"].at[0:15], a_peers)
    small_ref[...] = s["gathered_s"][...].reshape(RANKS * SMALL, 128)
    for copies in flights.values():
        for copy in copies:
            copy.wait_send()
    store_pressure.wait()
    store_gradient.wait()


def finish_kernel(
    pressure_in, pred_in, grad_in, small_in, pressure_out, pred_out, first, gain, second, head
):
    pressure_out[0] = pressure_in[...]
    for k in range(6):
        pred_out[0, :, lanes(k, 512)] = pred_in[k : k + 1, :].astype(BF16)
    for kx in range(3):
        for ky in range(3):
            for kz in range(3):
                k = (kx * 3 + ky) * 3 + kz
                second[kx, ky, kz] = grad_in[k].astype(F32)
                first[kx, ky, kz] = small_in[k * 3 : k * 3 + 3, 0:64]
    gain[...] = small_in[81:82, 0:64]
    head[...] = small_in[82:88, :]


def shards(
    velocity,
    first_kernel,
    norm_gain,
    second_kernel,
    head_weight,
    selection,
    assignment,
    target_stress,
):
    vmem = pl.BlockSpec(memory_space=pltpu.VMEM)
    smem = pl.BlockSpec(memory_space=pltpu.SMEM)
    anywhere = pl.BlockSpec(memory_space=pl.ANY)
    pressure, stress, grads, small = pl.pallas_call(
        kernel,
        out_shape=[
            jax.ShapeDtypeStruct((32, 32, 128), F32),
            jax.ShapeDtypeStruct((8, 512), F32),
            jax.ShapeDtypeStruct((TAPS, BIG, 128), BF16),
            jax.ShapeDtypeStruct((RANKS * SMALL, 128), F32),
        ],
        in_specs=[smem, smem, anywhere, vmem, vmem, anywhere, vmem, vmem],
        out_specs=[anywhere, vmem, anywhere, vmem],
        scratch_shapes=[pltpu.VMEM(shape, kind) for shape, kind in SCRATCH.values()]
        + [pltpu.SemaphoreType.DMA((n,)) for n in (SEMAPHORES, SEMAPHORES, 4)],
        compiler_params=pltpu.CompilerParams(
            collective_id=0, has_side_effects=True, vmem_limit_bytes=56 << 20
        ),
    )(
        selection,
        assignment.reshape(-1),
        velocity,
        first_kernel,
        norm_gain.reshape(1, 64),
        second_kernel,
        head_weight.T,
        target_stress,
    )
    pressure, predicted, first, gain, second, head = pl.pallas_call(
        finish_kernel,
        out_shape=[
            jax.ShapeDtypeStruct((1, 32, 32, 128), F32),
            jax.ShapeDtypeStruct((1, 1, 3072), BF16),
            jax.ShapeDtypeStruct((3, 3, 3, 3, 64), F32),
            jax.ShapeDtypeStruct((1, 64), F32),
            jax.ShapeDtypeStruct((3, 3, 3, 64, 128), F32),
            jax.ShapeDtypeStruct((6, 128), F32),
        ],
        in_specs=[vmem] * 4,
        out_specs=[vmem] * 6,
    )(pressure, stress, grads, small)
    return (pressure, predicted, first, gain.reshape(64), second, head.T)


def solution(mesh):
    placed = (
        P(("sec", "dom"), None, None, None, None),
        P(),
        P(),
        P(),
        P(),
        P(("sec", "dom"), None),
        P(),
        P(("sec", "dom"), None, None),
    )
    return jax.shard_map(
        shards,
        mesh=mesh,
        in_specs=placed,
        out_specs=(
            P(("sec", "dom"), None, None, None),
            P(("sec", "dom"), None, None),
            P(),
            P(),
            P(),
            P(),
        ),
        check_vma=False,
    )
```

```python
import jax
import jax.numpy as jnp
from jax import lax
from jax.experimental import pallas as pl
from jax.experimental.pallas import tpu as pltpu
from jax.sharding import PartitionSpec as P

F32 = jnp.float32
BF16 = jnp.bfloat16
NORM_EPS = 1e-05
MESH = pl.DeviceIdType.MESH
RANKS = 16
OWNERS = 32
TAPS = 27
BIG = 64
SMALL = 2


def iota(shape, dim):
    return lax.broadcasted_iota(jnp.int32, shape, dim)


def dot(left, right, cl, cr):
    return lax.dot_general(
        left, right, (((cl,), (cr,)), ((), ())), preferred_element_type=F32
    )


def lanes(t, width=128):
    return slice(t * width, (t + 1) * width)


def build_first_weights(sel, w1_ref, wg, table):
    for kx in range(3):
        for kz in range(3):
            rows = []
            for ky in range(3):
                w = w1_ref[kx, ky, kz].astype(F32)
                rows.append(jnp.concatenate([w, w], axis=1))
            for g in range(4):
                mixed = jnp.zeros((3, 128), F32)
                for ky in range(3):
                    mixed = jnp.where(lax.rem(sel + ky, 4) == g, rows[ky], mixed)
                for i in range(3):
                    wg[(kx * 3 + i) * 4 + g, kz : kz + 1, :] = mixed[i : i + 1]
    row = iota((32, 128), 0)
    upper = (iota((32, 128), 1) >= 64).astype(jnp.int32)
    for t in range(8):
        tap = row - 2 * (2 * t + upper) + 1
        masks = [(tap == k).astype(F32) for k in range(3)]

        for c in range(0, 36, 12):
            w = wg[c : c + 12]
            block = sum(masks[k][None] * w[:, k : k + 1, :] for k in range(3))
            table[c : c + 12, :, lanes(t)] = block.astype(BF16)


def build_rows(sel, vel_ref, mx):
    keep = lax.shift_right_logical(iota((8, 8, 128), 2), 5) == sel
    top = iota((8, 8, 128), 1) == 0
    for i in range(3):
        mx[i, 0, 0] = jnp.zeros((16, 128), BF16)
        for m in range(0, 16, 4):
            d = []
            for o in range(4):
                rows = vel_ref[i, 2 * m : 2 * m + 8, pl.ds(o, 8, stride=4), :]
                d.append(jnp.where(keep, rows, 0.0))
            before = jnp.where(top, 0.0, pltpu.roll(d[3], 1, 1))
            even = before + pltpu.roll(d[0], 32, 2) + pltpu.roll(d[1], 64, 2)
            odd = d[1] + pltpu.roll(d[2], 32, 2) + pltpu.roll(d[3], 64, 2)
            both = jnp.concatenate([even, odd], axis=1).astype(BF16)
            both = both.reshape(4, 2, 16, 128)
            mx[i, m : m + 4, 1] = both[:, 0]
            mx[i, m + 1 : m + 5, 0] = both[:, 1]


def first_rows(mx, kx, i):
    if kx == 0:
        part = mx[i, 0:16, 0]
    elif kx == 1:
        part = mx[i, 0:16, 1]
    else:
        part = mx[i, 1:17, 0]
    return part.reshape(256, 128)


def fold_channels(row):
    total = row[:, lanes(0)]
    for t in range(1, 8):
        total = total + row[:, lanes(t)]
    return total + pltpu.roll(total, 64, 1)


def first_layer(mx, table, cen):
    left = jnp.concatenate(
        [first_rows(mx, kx, i) for kx in range(3) for i in range(3)], axis=1
    )
    for t in range(4):
        right = table[:, :, lanes(t, 256)].reshape(1152, 256)
        cen[:, lanes(t, 256)] = dot(left, right, 1, 0)


def normalise(cen, gain_ref):
    total = fold_channels(jnp.sum(cen[...], axis=0, keepdims=True))
    mean = total * (1.0 / 4096.0)
    square = jnp.zeros((1, 128), F32)
    for t in range(8):
        c = cen[:, lanes(t)] - mean
        cen[:, lanes(t)] = c
        square = square + jnp.sum(c * c, axis=0, keepdims=True)
    var = (square + pltpu.roll(square, 64, 1)) * (1.0 / 4096.0)
    gain = gain_ref[0:1, :]
    gain = jnp.concatenate([gain, gain], axis=1)
    return gain, lax.rsqrt(var + NORM_EPS)


def hidden_rows(cen, scale, lhs):
    top = iota((16, 8, 128), 1) == 0
    for k in range(9):
        lhs[k, :, 0:128] = jnp.zeros((64, 128), BF16)
    for t in range(8):
        n = cen[:, lanes(t)] * scale
        h = (n * jax.nn.sigmoid(n)).reshape(16, 2, 8, 128)
        even, odd = h[:, 0], h[:, 1]
        before = jnp.where(top, 0.0, pltpu.roll(odd, 1, 1))
        for ky, plane in ((0, before), (1, even), (2, odd)):
            plane = plane.reshape(8, 2, 8, 128)
            low, high = plane[:, 0], plane[:, 1]
            shifted = jnp.concatenate([jnp.zeros((1, 8, 128), F32), high[:7]], axis=0)
            for kx, part in ((0, shifted), (1, low), (2, high)):
                lhs[kx * 3 + ky, :, lanes(t + 1)] = part.reshape(64, 128).astype(BF16)


def second_rows(lhs, k):
    return jnp.concatenate(
        [lhs[k, :, p * 128 : p * 128 + 256] for p in range(8)], axis=0
    )


def second_layer(lhs, wp):
    out = jnp.zeros((512, 128), F32)
    for k in range(9):
        out = out + dot(second_rows(lhs, k), wp[k // 3, k % 3].reshape(256, 128), 1, 0)
    return out


def cell_order():
    r, c = iota((512, 512), 0), iota((512, 512), 1)
    same = (lax.shift_right_logical(c, 3) == lax.bitwise_and(r, 63)) & (
        lax.bitwise_and(c, 7) == lax.shift_right_logical(r, 6)
    )
    return same.astype(F32).astype(BF16)


def target_rows(flat, wide):
    wide[...] = jnp.zeros((8, 768), F32)
    for k in range(6):
        wide[0:4, lanes(k)] = flat[4 * k : 4 * k + 4]
    row = iota((512, 8), 0)
    which = lax.bitwise_and(lax.shift_right_logical(row, 4), 3)
    pick = (which == iota((512, 8), 1)).astype(F32).astype(BF16)
    spread = dot(pick, wide[...].astype(BF16), 1, 0)
    row, lane = iota((512, 768), 0), iota((512, 768), 1)
    cell = (
        lax.bitwise_and(lax.shift_right_logical(row, 3), 1) * 64
        + lax.bitwise_and(row, 7) * 8
        + lax.shift_right_logical(row, 6)
    )
    kept = jnp.where(lax.bitwise_and(lane, 127) == cell, spread, 0.0).astype(BF16)
    r, c = iota((768, 128), 0), iota((768, 128), 1)
    collect = (lax.shift_right_logical(r, 7) == c).astype(F32).astype(BF16)
    return dot(kept, collect, 1, 0)


def second_gradient(lhs, dout, gb):
    for k in range(9):
        grad = dot(second_rows(lhs, k), dout, 0, 0)
        gb[k * 192 : (k + 1) * 192, :] = grad[64:256].astype(BF16)


def hidden_gradient(dout, wp, back):
    for k in range(9):
        back[k] = dot(dout, wp[k // 3, k % 3].reshape(256, 128), 1, 1)


def norm_backward(back, cen, gain, rstd, dn):
    scale = gain * rstd
    bottom = iota((8, 8, 128), 1) == 7
    sums = jnp.zeros((1, 128), F32)
    products = jnp.zeros((1, 128), F32)
    for t in range(8):
        planes = []
        for k in range(9):
            part = back[k, t * 64 : (t + 1) * 64, 128:256]
            if t < 7:
                part = part + back[k, (t + 1) * 64 : (t + 2) * 64, 0:128]
            planes.append(part.reshape(8, 8, 128))
        by_kx = []
        for kx in range(3):
            before = jnp.where(bottom, 0.0, pltpu.roll(planes[kx * 3], 7, 1))
            by_kx.append((planes[kx * 3 + 1], planes[kx * 3 + 2] + before))
        parts = []
        for q in range(2):
            moved = jnp.concatenate(
                [by_kx[0][q][1:], jnp.zeros((1, 8, 128), F32)], axis=0
            )
            parts.append((by_kx[1][q], by_kx[2][q] + moved))
        dh = jnp.stack(
            [
                jnp.stack([parts[0][0], parts[1][0]], axis=1),
                jnp.stack([parts[0][1], parts[1][1]], axis=1),
            ],
            axis=1,
        ).reshape(256, 128)
        dh = dh.astype(BF16).astype(F32)
        c = cen[:, lanes(t)]
        n = c * scale
        s = jax.nn.sigmoid(n)
        d = dh * (s * (1.0 + n * (1.0 - s)))
        dn[:, lanes(t)] = d
        sums = sums + jnp.sum(d, axis=0, keepdims=True)
        products = products + jnp.sum(d * c, axis=0, keepdims=True)
    sums = (sums + pltpu.roll(sums, 64, 1)) * (1.0 / 4096.0)
    products = products + pltpu.roll(products, 64, 1)
    slope = products * (rstd * rstd * (1.0 / 4096.0))
    for t in range(8):
        d = dn[:, lanes(t)]
        dn[:, lanes(t)] = scale * (d - sums - cen[:, lanes(t)] * slope)
    return products * rstd


def first_gradient(sel, mx, dn, gs):
    right = dn[...].astype(BF16)
    row = iota((128, 128), 0)
    z = lax.bitwise_and(row, 31)
    upper = (iota((128, 128), 1) >= 64).astype(jnp.int32)
    for kx in range(3):
        for i in range(3):
            full = dot(first_rows(mx, kx, i), right, 0, 0)
            for kz in range(3):
                total = jnp.zeros((128, 128), F32)
                for t in range(8):
                    tap = z - 2 * (2 * t + upper) + 1
                    total = total + jnp.where(tap == kz, full[:, lanes(t)], 0.0)
                total = jnp.sum(total.reshape(4, 32, 128), axis=1)
                total = total + pltpu.roll(total, 64, 1)
                for ky in range(3):
                    value = jnp.zeros((1, 128), F32)
                    for g in range(4):
                        value = jnp.where(
                            lax.rem(sel + ky, 4) == g, total[g : g + 1], value
                        )
                    at = ((kx * 3 + ky) * 3 + kz) * 3 + i
                    gs[at : at + 1, :] = value


def cell_masks(coords):
    _, by, bz = coords
    y, z = iota((40, 256), 0), iota((40, 256), 1)
    in_y = (y < 32) | ((y < 34) & (by < 3)) | ((y >= 38) & (by > 0))
    in_z = (z < 128) | ((z < 130) & (bz < 7)) | ((z >= 254) & (bz > 0))
    return jnp.where(in_y & in_z, 1.0 / 6.0, 0.0).astype(F32)


def divergence(vel_ref, rim_x, rim_y, rim_z, flags, window):
    first_row = iota((32, 128), 0) == 0
    first_lane = iota((32, 128), 1) == 0

    def layer(x, before):
        ux, uy, uz = vel_ref[0, x], vel_ref[1, x], vel_ref[2, x]
        y_rim = rim_y[x : x + 1, :] * flags[2]
        y_before = jnp.where(first_row, y_rim, pltpu.roll(uy, 1, 0))
        z_rim = pltpu.roll(rim_z[...], (128 - x) % 128, 1) * flags[4]
        z_before = jnp.where(first_lane, z_rim, pltpu.roll(uz, 1, 1))
        total = (ux - before) + (uy - y_before) + (uz - z_before)
        window[x + 2, 0:32, 0:128] = -total

    layer(0, rim_x[...] * flags[0])

    for x in range(1, 32):
        layer(x, vel_ref[0, x - 1])


def pack_rim_z(vel_ref, send):
    lane = iota((32, 128), 1)
    packed = jnp.zeros((32, 128), F32)
    for x in range(32):
        moved = pltpu.roll(vel_ref[2, x], (x + 1) % 128, 1)
        packed = jnp.where(lane == x, moved, packed)
    send[...] = packed


def pack_xy(field, h, send_x, send_y):
    send_x[0] = field[32 : 32 + h, 0:32, 0:128].astype(BF16)
    send_x[1] = field[h : 2 * h, 0:32, 0:128].astype(BF16)
    for r in range(h):
        send_y[0, r] = field[h : h + 32, 32 - h + r, 0:128].astype(BF16)
        send_y[1, r] = field[h : h + 32, r, 0:128].astype(BF16)


def unpack_xy(field, h, got_x, got_y, edges, flags):
    field[0:h, 0:32, 0:128] = got_x[0].astype(F32) * flags[0]
    field[h + 32 : h + 32 + h, 0:32, 0:128] = got_x[1].astype(F32) * flags[1]
    for side, at in ((0, 40 - h), (1, 32)):
        for r in range(h):
            row = at + r
            field[h : h + 32, row, 0:128] = got_y[side, r].astype(F32) * flags[2 + side]
            for end, low, take in ((0, 0, 16 - h), (1, h + 32, 0)):
                both = flags[2 + side] * flags[end]
                strip = edges[end * 2 + side, r].astype(F32) * both
                for k in range(h):
                    field[low + k, row : row + 1, 0:128] = strip[take + k : take + k + 1]


def pack_z(field, count, h, send):
    lane = iota((40, 128), 1)
    high = jnp.zeros((40, 128), F32)
    low = jnp.zeros((40, 128), F32)
    for x in range(count):
        here = (lane >= x * h) & (lane < x * h + h)
        own = field[x, :, 0:128]
        high = jnp.where(here, pltpu.roll(own, (x * h + h) % 128, 1), high)
        low = jnp.where(here, pltpu.roll(own, x * h, 1) if x else own, low)
    rest = jnp.zeros((8, 128), F32)
    send[0] = jnp.concatenate([high, rest], axis=0).astype(BF16)
    send[1] = jnp.concatenate([low, rest], axis=0).astype(BF16)


def unpack_z(field, count, h, got, flags):
    lane = iota((40, 128), 1)
    below = got[0, 0:40].astype(F32) * flags[4]
    above = got[1, 0:40].astype(F32) * flags[5]
    for x in range(count):
        lower = pltpu.roll(below, (128 - h - x * h) % 128, 1)
        upper = pltpu.roll(above, (-x * h) % 128, 1) if x else above
        field[x, :, 128:256] = jnp.where(
            lane < h, upper, jnp.where(lane >= 128 - h, lower, 0.0)
        )


def neighbours(field, at):
    own = field[at]
    across = field[at - 1] + field[at + 1]
    along = pltpu.roll(own, 1, 0) + pltpu.roll(own, 39, 0)
    return own, across + along + pltpu.roll(own, 1, 1) + pltpu.roll(own, 255, 1)


def local_solve(window, mask, za, zb, flags, pressure, emit):
    def inside(xi):
        if isinstance(xi, int):
            return flags[0] if xi < 2 else flags[1] if xi > 33 else 1.0
        return jnp.where(xi < 2, flags[0], jnp.where(xi > 33, flags[1], 1.0))

    for z in (za, zb):
        z[0] = jnp.zeros((40, 256), F32)
        z[37] = jnp.zeros((40, 256), F32)

    def first(xi):
        w = window[xi]
        if pressure is not None:
            own, around = neighbours(pressure, xi + 1)
            w = w - (6.0 * own - around)
            window[xi] = w
        za[xi + 1] = w * (mask[...] * inside(xi))

    def sweep(source, target):
        def step(xi):
            _, around = neighbours(source, xi + 1)
            target[xi + 1] = (window[xi] + around) * (mask[...] * inside(xi))

        return step

    def last(xi):
        _, around = neighbours(za, xi + 1)
        z = (window[xi] + around) * mask[...]
        emit(xi, z[0:32, 0:128])

    def over(low, high, body):
        half = (high - low) // 2

        def both(m, carry):
            for k in range(half):
                body(low + m * half + k)
            return carry

        lax.fori_loop(0, 2, both, 0)

    over(0, 36, first)
    over(0, 36, sweep(za, zb))
    over(1, 35, sweep(zb, za))
    over(2, 34, last)


SCRATCH = dict(
    wg=((36, 8, 128), F32),
    table=((36, 32, 1024), BF16),
    mx=((3, 17, 2, 16, 128), BF16),
    cen=((256, 1024), F32),
    lhs=((9, 64, 1152), BF16),
    wp=((3, 3, 4, 64, 128), BF16),
    vel=((3, 32, 32, 128), F32),
    done=((32, 32, 128), F32),
    hp=((128, 128), BF16),
    back=((9, 512, 256), F32),
    dn=((256, 1024), F32),
    wide=((8, 768), F32),
    rows=((32, 128), F32),
    t0=((32, 128), BF16),
    t1=((RANKS, 32, 128), BF16),
    stage=((RANKS, 32, 128), BF16),
    t2=((RANKS, 32, 128), BF16),
    gb=((OWNERS * BIG, 128), BF16),
    r1=((OWNERS, BIG, 128), BF16),
    parts=((8, BIG, 128), BF16),
    gathered=((OWNERS, BIG, 128), BF16),
    gs=((SMALL * BIG, 128), F32),
    gsb=((SMALL * BIG, 128), BF16),
    r1s=((OWNERS, BIG, 128), BF16),
    rim_x=((32, 128), F32),
    rim_y=((32, 128), F32),
    rim_z=((32, 128), F32),
    rim_ys=((32, 128), F32),
    rim_zs=((32, 128), F32),
    window=((36, 40, 256), F32),
    press=((38, 40, 256), F32),
    za=((38, 40, 256), F32),
    zb=((38, 40, 256), F32),
    mask=((40, 256), F32),
    wxs=((2, 2, 32, 128), BF16),
    wxr=((2, 2, 32, 128), BF16),
    wys=((2, 2, 32, 128), BF16),
    wyr=((2, 2, 32, 128), BF16),
    wer=((4, 2, 16, 128), BF16),
    wzs=((2, 48, 128), BF16),
    wzr=((2, 48, 128), BF16),
    pxs=((2, 3, 32, 128), BF16),
    pxr=((2, 3, 32, 128), BF16),
    pys=((2, 3, 32, 128), BF16),
    pyr=((2, 3, 32, 128), BF16),
    per=((4, 3, 16, 128), BF16),
    pzs=((2, 48, 128), BF16),
    pzr=((2, 48, 128), BF16),
)
GROUP_STEPS = ("t1", "t2", "g1", "g2", "g3", "s0", "s1")
HALO_STEPS = ("rim", "wxy", "wz", "pxy", "pz")
SEMAPHORES = len(GROUP_STEPS) + 8 * len(HALO_STEPS)


def kernel(*refs):
    (sel_ref, asg_ref, vel_hbm, w1_ref, gain_ref, w2_hbm, head_ref, target_ref) = refs[:8]
    pressure_ref, pred_ref, grad_ref = refs[8:11]
    s = dict(zip(SCRATCH, refs[11 : 11 + len(SCRATCH)]))
    send_sem, recv_sem, local_sem = refs[11 + len(SCRATCH) :]
    vel_ref = s["vel"]
    load_velocity = pltpu.make_async_copy(vel_hbm.at[0], vel_ref, local_sem.at[0])
    load_velocity.start()
    load_second = pltpu.make_async_copy(w2_hbm, s["wp"].at[:, :, 1:4], local_sem.at[1])
    load_second.start()

    me = lax.axis_index("sec") * 128 + lax.axis_index("dom")
    a, b = lax.div(me, 16), lax.rem(me, 16)
    z, core = lax.div(b, 2), lax.rem(b, 2)
    c = a * 2 + core
    coords = (lax.div(me, 32), lax.rem(lax.div(me, 8), 4), lax.rem(me, 8))
    bx, by, bz = coords
    flags = [
        jnp.where(cond, 1.0, 0.0).astype(F32)
        for cond in (bx > 0, bx < 7, by > 0, by < 3, bz > 0, bz < 7)
    ]

    def device(f):
        return (lax.div(f, 128), lax.rem(f, 128))

    def box(x, y, z):
        return device(
            lax.rem(bx + x + 8, 8) * 32 + lax.rem(by + y + 4, 4) * 8 + lax.rem(bz + z + 8, 8)
        )

    above = [box(1, 0, 0), box(0, 1, 0), box(0, 0, 1)]
    below = [box(-1, 0, 0), box(0, -1, 0), box(0, 0, -1)]
    corners = [box(1, 1, 0), box(1, -1, 0), box(-1, 1, 0), box(-1, -1, 0)]
    a_ranks = [None] + [lax.rem(a + j, RANKS) for j in range(1, RANKS)]
    b_ranks = [None] + [lax.rem(b + j, RANKS) for j in range(1, RANKS)]
    a_peers = [None] + [device(a_ranks[j] * 16 + b) for j in range(1, RANKS)]
    b_peers = [None] + [device(a * 16 + b_ranks[j]) for j in range(1, RANKS)]

    c_ranks = [None] + [lax.rem(c + j, OWNERS) for j in range(1, OWNERS)]
    c_peers = [None] + [
        device(lax.div(r, 2) * 16 + z * 2 + lax.rem(r, 2)) for r in c_ranks[1:]
    ]
    z_peers = [None] + [
        device(a * 16 + lax.rem(z + j, 8) * 2 + core) for j in range(1, 8)
    ]

    barrier = pltpu.get_barrier_semaphore()
    everyone = c_peers[1:] + b_peers[1:] + above + below + corners
    for other in everyone:
        pl.semaphore_signal(barrier, inc=1, device_id=other, device_id_type=MESH)

    flights = {}

    def remote(index, source, target, other):
        return pltpu.make_async_remote_copy(
            src_ref=source,
            dst_ref=target,
            send_sem=send_sem.at[index],
            recv_sem=recv_sem.at[index],
            device_id=other,
            device_id_type=MESH,
        )

    def start(step, at, source, target, other):
        index = len(GROUP_STEPS) + 8 * HALO_STEPS.index(step) + at
        copy = remote(index, source, target, other)
        copy.start()
        flights.setdefault(step, []).append(copy)

    def start_group(step, source, target, peers):
        for j in range(1, len(peers)):
            remote(GROUP_STEPS.index(step), source(j), target(j), peers[j]).start()

    def arrive_group(step, slots, peers):
        every = remote(GROUP_STEPS.index(step), slots, slots, peers[1])
        every.wait_recv()
        flights[step] = [every]

    def arrive(step):
        for copy in flights[step]:
            copy.wait_recv()

    def start_xy(step, field, h, send_x, got_x, send_y, got_y, edges):
        pack_xy(field, h, send_x, send_y)
        for k, (side, at) in enumerate(((0, 16), (1, 16), (0, 0), (1, 0))):
            start(step, 4 + k, send_y.at[side, :, at : at + 16, :], edges.at[k], corners[k])
        start(step, 2, send_y.at[0], got_y.at[0], above[1])
        start(step, 3, send_y.at[1], got_y.at[1], below[1])
        start(step, 0, send_x.at[0], got_x.at[0], above[0])
        start(step, 1, send_x.at[1], got_x.at[1], below[0])

    def start_z(step, send, got):
        start(step, 0, send.at[0], got.at[0], above[2])
        start(step, 1, send.at[1], got.at[1], below[2])

    sel = sel_ref[0, 0]
    window, press = s["window"], s["press"]
    flat = target_ref[0].astype(F32)
    s["rows"][...] = jnp.zeros((32, 128), F32)
    for r in range(24):
        s["rows"][r : r + 1, :] = flat[:, lanes(r)]
    s["t0"][...] = s["rows"][...].astype(BF16)
    s["t1"][a] = s["t0"][...]
    build_first_weights(sel, w1_ref, s["wg"], s["table"])
    load_velocity.wait()
    pack_rim_z(vel_ref, s["rim_zs"])
    s["rim_ys"][...] = vel_ref[1, :, 31, :]

    pl.semaphore_wait(barrier, len(everyone))

    start_group("t1", lambda j: s["t0"], lambda j: s["t1"].at[a], a_peers)
    start("rim", 0, vel_ref.at[0, 31], s["rim_x"], above[0])
    start("rim", 1, s["rim_ys"], s["rim_y"], above[1])
    start("rim", 2, s["rim_zs"], s["rim_z"], above[2])

    build_rows(sel, vel_ref, s["mx"])
    s["mask"][...] = cell_masks(coords)
    window[:, 32:40, 0:128] = jnp.zeros((36, 8, 128), F32)
    press[:, 32:40, 0:128] = jnp.zeros((38, 8, 128), F32)
    s["hp"][...] = jnp.zeros((128, 128), BF16)
    s["hp"][0:6, :] = head_ref[...]
    s["wp"][:, :, 0] = jnp.zeros((3, 3, 64, 128), BF16)
    s["gb"][TAPS * BIG :, :] = jnp.zeros(((OWNERS - TAPS) * BIG, 128), BF16)

    arrive_group("t1", s["t1"].at[0:15], a_peers)
    for q in range(RANKS):
        s["stage"][q] = s["t1"][lax.div(asg_ref[a * 16 + q], 16)]
    start_group("t2", lambda j: s["stage"].at[b_ranks[j]], lambda j: s["t2"].at[b], b_peers)
    s["t2"][b] = s["stage"][b]
    arrive("rim")
    divergence(vel_ref, s["rim_x"], s["rim_y"], s["rim_z"], flags, window)
    start_xy("wxy", window, 2, s["wxs"], s["wxr"], s["wys"], s["wyr"], s["wer"])

    first_layer(s["mx"], s["table"], s["cen"])
    gain, rstd = normalise(s["cen"], gain_ref)
    hidden_rows(s["cen"], gain * rstd, s["lhs"])
    load_second.wait()
    out = second_layer(s["lhs"], s["wp"])
    sig = jax.nn.sigmoid(out)
    deep = (out * sig).astype(BF16)
    slope = sig * (1.0 + out * (1.0 - sig))
    stress = dot(deep, s["hp"][...], 1, 1)

    arrive_group("t2", s["t2"].at[0:15], b_peers)
    target = s["t2"][lax.rem(asg_ref[me], 16)].astype(F32)
    error = (stress - target_rows(target, s["wide"])).astype(BF16)
    dout = dot(error, s["hp"][...], 1, 0).astype(BF16).astype(F32) * slope
    dout = dout.astype(BF16)
    second_gradient(s["lhs"], dout, s["gb"])

    def tap_rows(rank):
        return pl.ds(pl.multiple_of(rank * BIG, BIG), BIG)

    start_group(
        "g1", lambda j: s["gb"].at[tap_rows(c_ranks[j])], lambda j: s["r1"].at[j], c_peers
    )

    arrive("wxy")
    unpack_xy(window, 2, s["wxr"], s["wyr"], s["wer"], flags)
    pack_z(window, 36, 2, s["wzs"])
    start_z("wz", s["wzs"], s["wzr"])

    arrive("wz")
    unpack_z(window, 36, 2, s["wzr"], flags)

    def keep(xi, z):
        press[xi + 1, 0:32, 0:128] = z

    local_solve(window, s["mask"], s["za"], s["zb"], flags, None, keep)
    start_xy("pxy", press, 3, s["pxs"], s["pxr"], s["pys"], s["pyr"], s["per"])

    gs = s["gs"]
    gs[...] = jnp.zeros((128, 128), F32)
    gs[82:88, :] = dot(error, deep, 0, 0)[0:6]
    hidden_gradient(dout, s["wp"], s["back"])
    gs[81:82, :] = norm_backward(s["back"], s["cen"], gain, rstd, s["dn"])
    first_gradient(sel, s["mx"], s["dn"], gs)
    s["gsb"][...] = gs[...].astype(BF16)
    small_copies = []
    for n in range(SMALL):
        owner = TAPS + n
        rows = slice(n * BIG, (n + 1) * BIG)
        copy = pltpu.make_async_remote_copy(
            src_ref=s["gsb"].at[rows],
            dst_ref=s["r1s"].at[c],
            send_sem=send_sem.at[GROUP_STEPS.index("s0") + n],
            recv_sem=recv_sem.at[GROUP_STEPS.index("s0")],
            device_id=device(owner // 2 * 16 + z * 2 + owner % 2),
            device_id_type=MESH,
        )
        small_copies.append((owner, copy))

        @pl.when(c != owner)
        def _(copy=copy):
            copy.start()

        @pl.when(c == owner)
        def _(rows=rows):
            s["r1s"][c] = s["gsb"][rows, :]

    arrive_group("g1", s["r1"].at[1:OWNERS], c_peers)
    total = s["gb"][tap_rows(c), :].astype(F32)
    for j in range(1, OWNERS):
        total = total + s["r1"][j].astype(F32)
    s["parts"][z] = total.astype(BF16)

    @pl.when((c == TAPS) | (c == TAPS + 1))
    def _():
        slots = s["r1s"].at[0 : OWNERS - 1]
        remote(GROUP_STEPS.index("s0"), slots, slots, c_peers[1]).wait_recv()
        total = s["r1s"][0].astype(F32)
        for q in range(1, OWNERS):
            total = total + s["r1s"][q].astype(F32)
        s["parts"][z] = total.astype(BF16)

    start_group("g2", lambda j: s["parts"].at[z], lambda j: s["parts"].at[z], z_peers)
    pred_ref[...] = dot(stress.astype(BF16), cell_order(), 0, 0)[0:8]

    arrive("pxy")
    unpack_xy(press, 3, s["pxr"], s["pyr"], s["per"], flags)
    pack_z(press, 38, 3, s["pzs"])
    start_z("pz", s["pzs"], s["pzr"])

    arrive_group("g2", s["parts"].at[0:7], z_peers)
    total = s["parts"][0].astype(F32)
    for q in range(1, 8):
        total = total + s["parts"][q].astype(F32)
    gathered = s["gathered"]
    gathered[c] = total.astype(BF16)
    start_group("g3", lambda j: gathered.at[c], lambda j: gathered.at[c], c_peers)

    arrive("pz")
    unpack_z(press, 38, 3, s["pzr"], flags)

    def finish(xi, z):
        s["done"][xi - 2] = press[xi + 1, 0:32, 0:128] + z

    local_solve(window, s["mask"], s["za"], s["zb"], flags, press, finish)
    store_pressure = pltpu.make_async_copy(s["done"], pressure_ref, local_sem.at[2])
    store_pressure.start()

    arrive_group("g3", gathered.at[0 : OWNERS - 1], c_peers)
    store_gradient = pltpu.make_async_copy(
        gathered.at[0 : TAPS + SMALL], grad_ref, local_sem.at[3]
    )
    store_gradient.start()
    for copies in flights.values():
        for copy in copies:
            copy.wait_send()
    for owner, copy in small_copies:

        @pl.when(c != owner)
        def _(copy=copy):
            copy.wait_send()

    store_pressure.wait()
    store_gradient.wait()


def finish_kernel(
    pressure_in, pred_in, grad_in, pressure_out, pred_out, first, gain, second, head, small_in
):
    small_in[...] = grad_in[TAPS : TAPS + SMALL].reshape(SMALL * BIG, 128).astype(F32)
    pressure_out[0] = pressure_in[...]
    for k in range(6):
        pred_out[0, :, lanes(k, 512)] = pred_in[k : k + 1, :].astype(BF16)
    for kx in range(3):
        for ky in range(3):
            for kz in range(3):
                k = (kx * 3 + ky) * 3 + kz
                second[kx, ky, kz] = grad_in[k].astype(F32)
                first[kx, ky, kz] = small_in[k * 3 : k * 3 + 3, 0:64]
    gain[...] = small_in[81:82, 0:64]
    head[...] = small_in[82:88, :]


def shards(
    velocity,
    first_kernel,
    norm_gain,
    second_kernel,
    head_weight,
    selection,
    assignment,
    target_stress,
):
    vmem = pl.BlockSpec(memory_space=pltpu.VMEM)
    smem = pl.BlockSpec(memory_space=pltpu.SMEM)
    anywhere = pl.BlockSpec(memory_space=pl.ANY)
    pressure, stress, grads = pl.pallas_call(
        kernel,
        out_shape=[
            jax.ShapeDtypeStruct((32, 32, 128), F32),
            jax.ShapeDtypeStruct((8, 512), F32),
            jax.ShapeDtypeStruct((TAPS + SMALL, BIG, 128), BF16),
        ],
        in_specs=[smem, smem, anywhere, vmem, vmem, anywhere, vmem, vmem],
        out_specs=[anywhere, vmem, anywhere],
        scratch_shapes=[pltpu.VMEM(shape, kind) for shape, kind in SCRATCH.values()]
        + [pltpu.SemaphoreType.DMA((n,)) for n in (SEMAPHORES, SEMAPHORES, 4)],
        compiler_params=pltpu.CompilerParams(
            collective_id=0, has_side_effects=True, vmem_limit_bytes=56 << 20
        ),
    )(
        selection,
        assignment.reshape(-1),
        velocity,
        first_kernel,
        norm_gain.reshape(1, 64),
        second_kernel,
        head_weight.T,
        target_stress,
    )
    pressure, predicted, first, gain, second, head = pl.pallas_call(
        finish_kernel,
        out_shape=[
            jax.ShapeDtypeStruct((1, 32, 32, 128), F32),
            jax.ShapeDtypeStruct((1, 1, 3072), BF16),
            jax.ShapeDtypeStruct((3, 3, 3, 3, 64), F32),
            jax.ShapeDtypeStruct((1, 64), F32),
            jax.ShapeDtypeStruct((3, 3, 3, 64, 128), F32),
            jax.ShapeDtypeStruct((6, 128), F32),
        ],
        in_specs=[vmem] * 3,
        out_specs=[vmem] * 6,
        scratch_shapes=[pltpu.VMEM((SMALL * BIG, 128), F32)],
    )(pressure, stress, grads)
    return (pressure, predicted, first, gain.reshape(64), second, head.T)


def solution(mesh):
    placed = (
        P(("sec", "dom"), None, None, None, None),
        P(),
        P(),
        P(),
        P(),
        P(("sec", "dom"), None),
        P(),
        P(("sec", "dom"), None, None),
    )
    return jax.shard_map(
        shards,
        mesh=mesh,
        in_specs=placed,
        out_specs=(
            P(("sec", "dom"), None, None, None),
            P(("sec", "dom"), None, None),
            P(),
            P(),
            P(),
            P(),
        ),
        check_vma=False,
    )
```

```python
import jax
import jax.numpy as jnp
from jax import lax
from jax.experimental import pallas as pl
from jax.experimental.pallas import tpu as pltpu
from jax.sharding import PartitionSpec as P

F32 = jnp.float32
BF16 = jnp.bfloat16
NORM_EPS = 1e-05
MESH = pl.DeviceIdType.MESH
RANKS = 16
OWNERS = 32
TAPS = 27
BIG = 64
SMALL = 2


def iota(shape, dim):
    return lax.broadcasted_iota(jnp.int32, shape, dim)


def dot(left, right, cl, cr):
    return lax.dot_general(
        left, right, (((cl,), (cr,)), ((), ())), preferred_element_type=F32
    )


def lanes(t, width=128):
    return slice(t * width, (t + 1) * width)


def build_first_weights(sel, w1_ref, wg, table):
    for kx in range(3):
        for kz in range(3):
            rows = []
            for ky in range(3):
                w = w1_ref[kx, ky, kz].astype(F32)
                rows.append(jnp.concatenate([w, w], axis=1))
            for g in range(4):
                mixed = jnp.zeros((3, 128), F32)
                for ky in range(3):
                    mixed = jnp.where(lax.rem(sel + ky, 4) == g, rows[ky], mixed)
                for i in range(3):
                    wg[(kx * 3 + i) * 4 + g, kz : kz + 1, :] = mixed[i : i + 1]
    row = iota((32, 128), 0)
    upper = (iota((32, 128), 1) >= 64).astype(jnp.int32)
    for t in range(8):
        tap = row - 2 * (2 * t + upper) + 1
        masks = [(tap == k).astype(F32) for k in range(3)]

        for c in range(0, 36, 12):
            w = wg[c : c + 12]
            block = sum(masks[k][None] * w[:, k : k + 1, :] for k in range(3))
            table[c : c + 12, :, lanes(t)] = block.astype(BF16)


def build_rows(sel, vel_ref, mx):
    keep = lax.shift_right_logical(iota((8, 8, 128), 2), 5) == sel
    top = iota((8, 8, 128), 1) == 0
    for i in range(3):
        mx[i, 0, 0] = jnp.zeros((16, 128), BF16)
        for m in range(0, 16, 4):
            d = []
            for o in range(4):
                rows = vel_ref[i, 2 * m : 2 * m + 8, pl.ds(o, 8, stride=4), :]
                d.append(jnp.where(keep, rows, 0.0))
            before = jnp.where(top, 0.0, pltpu.roll(d[3], 1, 1))
            even = before + pltpu.roll(d[0], 32, 2) + pltpu.roll(d[1], 64, 2)
            odd = d[1] + pltpu.roll(d[2], 32, 2) + pltpu.roll(d[3], 64, 2)
            both = jnp.concatenate([even, odd], axis=1).astype(BF16)
            both = both.reshape(4, 2, 16, 128)
            mx[i, m : m + 4, 1] = both[:, 0]
            mx[i, m + 1 : m + 5, 0] = both[:, 1]


def first_rows(mx, kx, i):
    if kx == 0:
        part = mx[i, 0:16, 0]
    elif kx == 1:
        part = mx[i, 0:16, 1]
    else:
        part = mx[i, 1:17, 0]
    return part.reshape(256, 128)


def fold_channels(row):
    total = row[:, lanes(0)]
    for t in range(1, 8):
        total = total + row[:, lanes(t)]
    return total + pltpu.roll(total, 64, 1)


def first_layer(mx, table, cen):
    left = jnp.concatenate(
        [first_rows(mx, kx, i) for kx in range(3) for i in range(3)], axis=1
    )
    for t in range(4):
        right = table[:, :, lanes(t, 256)].reshape(1152, 256)
        cen[:, lanes(t, 256)] = dot(left, right, 1, 0)


def normalise(cen, gain_ref):
    total = fold_channels(jnp.sum(cen[...], axis=0, keepdims=True))
    mean = total * (1.0 / 4096.0)
    square = jnp.zeros((1, 128), F32)
    for t in range(8):
        c = cen[:, lanes(t)] - mean
        cen[:, lanes(t)] = c
        square = square + jnp.sum(c * c, axis=0, keepdims=True)
    var = (square + pltpu.roll(square, 64, 1)) * (1.0 / 4096.0)
    gain = gain_ref[0:1, :]
    gain = jnp.concatenate([gain, gain], axis=1)
    return gain, lax.rsqrt(var + NORM_EPS)


def hidden_rows(cen, scale, lhs):
    top = iota((16, 8, 128), 1) == 0
    for k in range(9):
        lhs[k, :, 0:128] = jnp.zeros((64, 128), BF16)
    for t in range(8):
        n = cen[:, lanes(t)] * scale
        h = (n * jax.nn.sigmoid(n)).reshape(16, 2, 8, 128)
        even, odd = h[:, 0], h[:, 1]
        before = jnp.where(top, 0.0, pltpu.roll(odd, 1, 1))
        for ky, plane in ((0, before), (1, even), (2, odd)):
            plane = plane.reshape(8, 2, 8, 128)
            low, high = plane[:, 0], plane[:, 1]
            shifted = jnp.concatenate([jnp.zeros((1, 8, 128), F32), high[:7]], axis=0)
            for kx, part in ((0, shifted), (1, low), (2, high)):
                lhs[kx * 3 + ky, :, lanes(t + 1)] = part.reshape(64, 128).astype(BF16)


def second_rows(lhs, k):
    return jnp.concatenate(
        [lhs[k, :, p * 128 : p * 128 + 256] for p in range(8)], axis=0
    )


def second_layer(lhs, wp):
    out = jnp.zeros((512, 128), F32)
    for k in range(9):
        out = out + dot(second_rows(lhs, k), wp[k // 3, k % 3].reshape(256, 128), 1, 0)
    return out


def cell_order():
    r, c = iota((512, 512), 0), iota((512, 512), 1)
    same = (lax.shift_right_logical(c, 3) == lax.bitwise_and(r, 63)) & (
        lax.bitwise_and(c, 7) == lax.shift_right_logical(r, 6)
    )
    return same.astype(F32).astype(BF16)


def target_rows(flat, wide):
    wide[...] = jnp.zeros((8, 768), F32)
    for k in range(6):
        wide[0:4, lanes(k)] = flat[4 * k : 4 * k + 4]
    row = iota((512, 8), 0)
    which = lax.bitwise_and(lax.shift_right_logical(row, 4), 3)
    pick = (which == iota((512, 8), 1)).astype(F32).astype(BF16)
    spread = dot(pick, wide[...].astype(BF16), 1, 0)
    row, lane = iota((512, 768), 0), iota((512, 768), 1)
    cell = (
        lax.bitwise_and(lax.shift_right_logical(row, 3), 1) * 64
        + lax.bitwise_and(row, 7) * 8
        + lax.shift_right_logical(row, 6)
    )
    kept = jnp.where(lax.bitwise_and(lane, 127) == cell, spread, 0.0).astype(BF16)
    r, c = iota((768, 128), 0), iota((768, 128), 1)
    collect = (lax.shift_right_logical(r, 7) == c).astype(F32).astype(BF16)
    return dot(kept, collect, 1, 0)


def second_gradient(lhs, dout, gb):
    for k in range(9):
        grad = dot(second_rows(lhs, k), dout, 0, 0)
        gb[k * 192 : (k + 1) * 192, :] = grad[64:256].astype(BF16)


def hidden_gradient(dout, wp, back):
    for k in range(9):
        back[k] = dot(dout, wp[k // 3, k % 3].reshape(256, 128), 1, 1)


def norm_backward(back, cen, gain, rstd, dn):
    scale = gain * rstd
    bottom = iota((8, 8, 128), 1) == 7
    sums = jnp.zeros((1, 128), F32)
    products = jnp.zeros((1, 128), F32)
    for t in range(8):
        planes = []
        for k in range(9):
            part = back[k, t * 64 : (t + 1) * 64, 128:256]
            if t < 7:
                part = part + back[k, (t + 1) * 64 : (t + 2) * 64, 0:128]
            planes.append(part.reshape(8, 8, 128))
        by_kx = []
        for kx in range(3):
            before = jnp.where(bottom, 0.0, pltpu.roll(planes[kx * 3], 7, 1))
            by_kx.append((planes[kx * 3 + 1], planes[kx * 3 + 2] + before))
        parts = []
        for q in range(2):
            moved = jnp.concatenate(
                [by_kx[0][q][1:], jnp.zeros((1, 8, 128), F32)], axis=0
            )
            parts.append((by_kx[1][q], by_kx[2][q] + moved))
        dh = jnp.stack(
            [
                jnp.stack([parts[0][0], parts[1][0]], axis=1),
                jnp.stack([parts[0][1], parts[1][1]], axis=1),
            ],
            axis=1,
        ).reshape(256, 128)
        dh = dh.astype(BF16).astype(F32)
        c = cen[:, lanes(t)]
        n = c * scale
        s = jax.nn.sigmoid(n)
        d = dh * (s * (1.0 + n * (1.0 - s)))
        dn[:, lanes(t)] = d
        sums = sums + jnp.sum(d, axis=0, keepdims=True)
        products = products + jnp.sum(d * c, axis=0, keepdims=True)
    sums = (sums + pltpu.roll(sums, 64, 1)) * (1.0 / 4096.0)
    products = products + pltpu.roll(products, 64, 1)
    slope = products * (rstd * rstd * (1.0 / 4096.0))
    for t in range(8):
        d = dn[:, lanes(t)]
        dn[:, lanes(t)] = scale * (d - sums - cen[:, lanes(t)] * slope)
    return products * rstd


def first_gradient(sel, mx, dn, gs):
    right = dn[...].astype(BF16)
    row = iota((128, 128), 0)
    z = lax.bitwise_and(row, 31)
    upper = (iota((128, 128), 1) >= 64).astype(jnp.int32)
    for kx in range(3):
        for i in range(3):
            full = dot(first_rows(mx, kx, i), right, 0, 0)
            for kz in range(3):
                total = jnp.zeros((128, 128), F32)
                for t in range(8):
                    tap = z - 2 * (2 * t + upper) + 1
                    total = total + jnp.where(tap == kz, full[:, lanes(t)], 0.0)
                total = jnp.sum(total.reshape(4, 32, 128), axis=1)
                total = total + pltpu.roll(total, 64, 1)
                for ky in range(3):
                    value = jnp.zeros((1, 128), F32)
                    for g in range(4):
                        value = jnp.where(
                            lax.rem(sel + ky, 4) == g, total[g : g + 1], value
                        )
                    at = ((kx * 3 + ky) * 3 + kz) * 3 + i
                    gs[at : at + 1, :] = value


def cell_masks(coords):
    _, by, bz = coords
    y, z = iota((40, 256), 0), iota((40, 256), 1)
    in_y = (y < 32) | ((y < 34) & (by < 3)) | ((y >= 38) & (by > 0))
    in_z = (z < 128) | ((z < 130) & (bz < 7)) | ((z >= 254) & (bz > 0))
    return jnp.where(in_y & in_z, 1.0 / 6.0, 0.0).astype(F32)


def divergence(vel_ref, rim_x, rim_y, rim_z, flags, window):
    first_row = iota((32, 128), 0) == 0
    first_lane = iota((32, 128), 1) == 0

    def layer(x, before):
        ux, uy, uz = vel_ref[0, x], vel_ref[1, x], vel_ref[2, x]
        y_rim = rim_y[x : x + 1, :] * flags[2]
        y_before = jnp.where(first_row, y_rim, pltpu.roll(uy, 1, 0))
        z_rim = pltpu.roll(rim_z[...], (128 - x) % 128, 1) * flags[4]
        z_before = jnp.where(first_lane, z_rim, pltpu.roll(uz, 1, 1))
        total = (ux - before) + (uy - y_before) + (uz - z_before)
        window[x + 2, 0:32, 0:128] = -total

    layer(0, rim_x[...] * flags[0])

    for x in range(1, 32):
        layer(x, vel_ref[0, x - 1])


def pack_rim_z(vel_ref, send):
    lane = iota((32, 128), 1)
    packed = jnp.zeros((32, 128), F32)
    for x in range(32):
        moved = pltpu.roll(vel_ref[2, x], (x + 1) % 128, 1)
        packed = jnp.where(lane == x, moved, packed)
    send[...] = packed


def pack_xy(field, h, send_x, send_y, send_e, edge):
    for k, (x, y) in enumerate(((32, 32 - h), (32, 0), (h, 32 - h), (h, 0))):
        edge[...] = jnp.zeros((16, 128), F32)
        for r in range(h):
            for m in range(h):
                edge[r * h + m : r * h + m + 1, :] = field[x + m, y + r : y + r + 1, 0:128]
        send_e[k] = edge[...].astype(BF16)
    send_x[0] = field[32 : 32 + h, 0:32, 0:128].astype(BF16)
    send_x[1] = field[h : 2 * h, 0:32, 0:128].astype(BF16)
    for r in range(h):
        send_y[0, r] = field[h : h + 32, 32 - h + r, 0:128].astype(BF16)
        send_y[1, r] = field[h : h + 32, r, 0:128].astype(BF16)


def unpack_xy(field, h, got_x, got_y, edges, flags):
    field[0:h, 0:32, 0:128] = got_x[0].astype(F32) * flags[0]
    field[h + 32 : h + 32 + h, 0:32, 0:128] = got_x[1].astype(F32) * flags[1]
    for side, at in ((0, 40 - h), (1, 32)):
        for r in range(h):
            row = at + r
            field[h : h + 32, row, 0:128] = got_y[side, r].astype(F32) * flags[2 + side]
            for end, low in ((0, 0), (1, h + 32)):
                both = flags[2 + side] * flags[end]
                strip = edges[end * 2 + side].astype(F32) * both
                for k in range(h):
                    field[low + k, row : row + 1, 0:128] = strip[r * h + k : r * h + k + 1]


def pack_z(field, count, h, send):
    lane = iota((40, 128), 1)
    high = jnp.zeros((40, 128), F32)
    low = jnp.zeros((40, 128), F32)
    for x in range(count):
        here = (lane >= x * h) & (lane < x * h + h)
        own = field[x, :, 0:128]
        high = jnp.where(here, pltpu.roll(own, (x * h + h) % 128, 1), high)
        low = jnp.where(here, pltpu.roll(own, x * h, 1) if x else own, low)
    rest = jnp.zeros((8, 128), F32)
    send[0] = jnp.concatenate([high, rest], axis=0).astype(BF16)
    send[1] = jnp.concatenate([low, rest], axis=0).astype(BF16)


def unpack_z(field, count, h, got, flags):
    lane = iota((40, 128), 1)
    below = got[0, 0:40].astype(F32) * flags[4]
    above = got[1, 0:40].astype(F32) * flags[5]
    for x in range(count):
        lower = pltpu.roll(below, (128 - h - x * h) % 128, 1)
        upper = pltpu.roll(above, (-x * h) % 128, 1) if x else above
        field[x, :, 128:256] = jnp.where(
            lane < h, upper, jnp.where(lane >= 128 - h, lower, 0.0)
        )


def neighbours(field, at):
    own = field[at]
    across = field[at - 1] + field[at + 1]
    along = pltpu.roll(own, 1, 0) + pltpu.roll(own, 39, 0)
    return own, across + along + pltpu.roll(own, 1, 1) + pltpu.roll(own, 255, 1)


def local_solve(window, mask, za, zb, flags, pressure, emit):
    def inside(xi):
        return flags[0] if xi < 2 else flags[1] if xi > 33 else 1.0

    for z in (za, zb):
        z[0] = jnp.zeros((40, 256), F32)
        z[37] = jnp.zeros((40, 256), F32)

    def first(xi):
        w = window[xi]
        if pressure is not None:
            own, around = neighbours(pressure, xi + 1)
            w = w - (6.0 * own - around)
            window[xi] = w
        za[xi + 1] = w * (mask[...] * inside(xi))

    def sweep(source, target):
        def step(xi):
            _, around = neighbours(source, xi + 1)
            target[xi + 1] = (window[xi] + around) * (mask[...] * inside(xi))

        return step

    def last(xi):
        _, around = neighbours(za, xi + 1)
        z = (window[xi] + around) * mask[...]
        emit(xi, z[0:32, 0:128])

    def over(low, high, body):
        for xi in range(low, high):
            body(xi)

    over(0, 36, first)
    over(0, 36, sweep(za, zb))
    over(1, 35, sweep(zb, za))
    over(2, 34, last)


SCRATCH = dict(
    wg=((36, 8, 128), F32),
    table=((36, 32, 1024), BF16),
    mx=((3, 17, 2, 16, 128), BF16),
    cen=((256, 1024), F32),
    lhs=((9, 64, 1152), BF16),
    wp=((3, 3, 4, 64, 128), BF16),
    vel=((3, 32, 32, 128), F32),
    done=((32, 32, 128), F32),
    hp=((128, 128), BF16),
    back=((9, 512, 256), F32),
    dn=((256, 1024), F32),
    wide=((8, 768), F32),
    rows=((32, 128), F32),
    t0=((32, 128), BF16),
    t1=((RANKS, 32, 128), BF16),
    stage=((RANKS, 32, 128), BF16),
    t2=((RANKS, 32, 128), BF16),
    gb=((OWNERS * BIG, 128), BF16),
    r1=((OWNERS, BIG, 128), BF16),
    parts=((8, BIG, 128), BF16),
    gathered=((OWNERS, BIG, 128), BF16),
    gs=((SMALL * BIG, 128), F32),
    gsb=((SMALL * BIG, 128), BF16),
    r1s=((OWNERS, BIG, 128), BF16),
    rim_x=((32, 128), F32),
    rim_y=((32, 128), F32),
    rim_z=((32, 128), F32),
    rim_ys=((32, 128), F32),
    rim_zs=((32, 128), F32),
    window=((36, 40, 256), F32),
    press=((38, 40, 256), F32),
    za=((38, 40, 256), F32),
    zb=((38, 40, 256), F32),
    mask=((40, 256), F32),
    edge=((16, 128), F32),
    wxs=((2, 2, 32, 128), BF16),
    wxr=((2, 2, 32, 128), BF16),
    wys=((2, 2, 32, 128), BF16),
    wyr=((2, 2, 32, 128), BF16),
    wes=((4, 16, 128), BF16),
    wer=((4, 16, 128), BF16),
    wzs=((2, 48, 128), BF16),
    wzr=((2, 48, 128), BF16),
    pxs=((2, 3, 32, 128), BF16),
    pxr=((2, 3, 32, 128), BF16),
    pys=((2, 3, 32, 128), BF16),
    pyr=((2, 3, 32, 128), BF16),
    pes=((4, 16, 128), BF16),
    per=((4, 16, 128), BF16),
    pzs=((2, 48, 128), BF16),
    pzr=((2, 48, 128), BF16),
)
GROUP_STEPS = ("t1", "t2", "g1", "g2", "g3", "s0", "s1")
HALO_STEPS = ("rim", "wxy", "wz", "pxy", "pz")
SEMAPHORES = len(GROUP_STEPS) + 8 * len(HALO_STEPS)


def kernel(*refs):
    (sel_ref, asg_ref, vel_hbm, w1_ref, gain_ref, w2_hbm, head_ref, target_ref) = refs[:8]
    pressure_ref, pred_ref, grad_ref = refs[8:11]
    s = dict(zip(SCRATCH, refs[11 : 11 + len(SCRATCH)]))
    send_sem, recv_sem, local_sem = refs[11 + len(SCRATCH) :]
    vel_ref = s["vel"]
    load_velocity = pltpu.make_async_copy(vel_hbm.at[0], vel_ref, local_sem.at[0])
    load_velocity.start()
    load_second = pltpu.make_async_copy(w2_hbm, s["wp"].at[:, :, 1:4], local_sem.at[1])
    load_second.start()

    me = lax.axis_index("sec") * 128 + lax.axis_index("dom")
    a, b = lax.div(me, 16), lax.rem(me, 16)
    z, core = lax.div(b, 2), lax.rem(b, 2)
    c = a * 2 + core
    coords = (lax.div(me, 32), lax.rem(lax.div(me, 8), 4), lax.rem(me, 8))
    bx, by, bz = coords
    flags = [
        jnp.where(cond, 1.0, 0.0).astype(F32)
        for cond in (bx > 0, bx < 7, by > 0, by < 3, bz > 0, bz < 7)
    ]

    def device(f):
        return (lax.div(f, 128), lax.rem(f, 128))

    def box(x, y, z):
        return device(
            lax.rem(bx + x + 8, 8) * 32 + lax.rem(by + y + 4, 4) * 8 + lax.rem(bz + z + 8, 8)
        )

    above = [box(1, 0, 0), box(0, 1, 0), box(0, 0, 1)]
    below = [box(-1, 0, 0), box(0, -1, 0), box(0, 0, -1)]
    corners = [box(1, 1, 0), box(1, -1, 0), box(-1, 1, 0), box(-1, -1, 0)]
    a_ranks = [None] + [lax.rem(a + j, RANKS) for j in range(1, RANKS)]
    b_ranks = [None] + [lax.rem(b + j, RANKS) for j in range(1, RANKS)]
    a_peers = [None] + [device(a_ranks[j] * 16 + b) for j in range(1, RANKS)]
    b_peers = [None] + [device(a * 16 + b_ranks[j]) for j in range(1, RANKS)]

    c_ranks = [None] + [lax.rem(c + j, OWNERS) for j in range(1, OWNERS)]
    c_peers = [None] + [
        device(lax.div(r, 2) * 16 + z * 2 + lax.rem(r, 2)) for r in c_ranks[1:]
    ]
    z_peers = [None] + [
        device(a * 16 + lax.rem(z + j, 8) * 2 + core) for j in range(1, 8)
    ]

    barrier = pltpu.get_barrier_semaphore()
    everyone = c_peers[1:] + b_peers[1:] + above + below + corners
    for other in everyone:
        pl.semaphore_signal(barrier, inc=1, device_id=other, device_id_type=MESH)

    flights = {}

    def remote(index, source, target, other):
        return pltpu.make_async_remote_copy(
            src_ref=source,
            dst_ref=target,
            send_sem=send_sem.at[index],
            recv_sem=recv_sem.at[index],
            device_id=other,
            device_id_type=MESH,
        )

    def start(step, at, source, target, other):
        index = len(GROUP_STEPS) + 8 * HALO_STEPS.index(step) + at
        copy = remote(index, source, target, other)
        copy.start()
        flights.setdefault(step, []).append(copy)

    def start_group(step, source, target, peers):
        for j in range(1, len(peers)):
            remote(GROUP_STEPS.index(step), source(j), target(j), peers[j]).start()

    def arrive_group(step, slots, peers):
        every = remote(GROUP_STEPS.index(step), slots, slots, peers[1])
        every.wait_recv()
        flights[step] = [every]

    def arrive(step):
        for copy in flights[step]:
            copy.wait_recv()

    def start_xy(step, field, h, send_x, got_x, send_y, got_y, send_e, edges):
        pack_xy(field, h, send_x, send_y, send_e, s["edge"])
        for k in range(4):
            start(step, 4 + k, send_e.at[k], edges.at[k], corners[k])
        start(step, 2, send_y.at[0], got_y.at[0], above[1])
        start(step, 3, send_y.at[1], got_y.at[1], below[1])
        start(step, 0, send_x.at[0], got_x.at[0], above[0])
        start(step, 1, send_x.at[1], got_x.at[1], below[0])

    def start_z(step, send, got):
        start(step, 0, send.at[0], got.at[0], above[2])
        start(step, 1, send.at[1], got.at[1], below[2])

    sel = sel_ref[0, 0]
    window, press = s["window"], s["press"]
    flat = target_ref[0].astype(F32)
    s["rows"][...] = jnp.zeros((32, 128), F32)
    for r in range(24):
        s["rows"][r : r + 1, :] = flat[:, lanes(r)]
    s["t0"][...] = s["rows"][...].astype(BF16)
    s["t1"][a] = s["t0"][...]
    build_first_weights(sel, w1_ref, s["wg"], s["table"])
    load_velocity.wait()
    pack_rim_z(vel_ref, s["rim_zs"])
    s["rim_ys"][...] = vel_ref[1, :, 31, :]

    pl.semaphore_wait(barrier, len(everyone))

    start_group("t1", lambda j: s["t0"], lambda j: s["t1"].at[a], a_peers)
    start("rim", 0, vel_ref.at[0, 31], s["rim_x"], above[0])
    start("rim", 1, s["rim_ys"], s["rim_y"], above[1])
    start("rim", 2, s["rim_zs"], s["rim_z"], above[2])

    build_rows(sel, vel_ref, s["mx"])
    s["mask"][...] = cell_masks(coords)
    window[:, 32:40, 0:128] = jnp.zeros((36, 8, 128), F32)
    press[:, 32:40, 0:128] = jnp.zeros((38, 8, 128), F32)
    s["hp"][...] = jnp.zeros((128, 128), BF16)
    s["hp"][0:6, :] = head_ref[...]
    s["wp"][:, :, 0] = jnp.zeros((3, 3, 64, 128), BF16)
    s["gb"][TAPS * BIG :, :] = jnp.zeros(((OWNERS - TAPS) * BIG, 128), BF16)

    arrive_group("t1", s["t1"].at[0:15], a_peers)
    for q in range(RANKS):
        s["stage"][q] = s["t1"][lax.div(asg_ref[a * 16 + q], 16)]
    start_group("t2", lambda j: s["stage"].at[b_ranks[j]], lambda j: s["t2"].at[b], b_peers)
    s["t2"][b] = s["stage"][b]
    arrive("rim")
    divergence(vel_ref, s["rim_x"], s["rim_y"], s["rim_z"], flags, window)
    start_xy(
        "wxy", window, 2, s["wxs"], s["wxr"], s["wys"], s["wyr"], s["wes"], s["wer"]
    )

    first_layer(s["mx"], s["table"], s["cen"])
    gain, rstd = normalise(s["cen"], gain_ref)
    hidden_rows(s["cen"], gain * rstd, s["lhs"])
    load_second.wait()
    out = second_layer(s["lhs"], s["wp"])
    sig = jax.nn.sigmoid(out)
    deep = (out * sig).astype(BF16)
    slope = sig * (1.0 + out * (1.0 - sig))
    stress = dot(deep, s["hp"][...], 1, 1)

    arrive_group("t2", s["t2"].at[0:15], b_peers)
    target = s["t2"][lax.rem(asg_ref[me], 16)].astype(F32)
    error = (stress - target_rows(target, s["wide"])).astype(BF16)
    dout = dot(error, s["hp"][...], 1, 0).astype(BF16).astype(F32) * slope
    dout = dout.astype(BF16)
    second_gradient(s["lhs"], dout, s["gb"])

    def tap_rows(rank):
        return pl.ds(pl.multiple_of(rank * BIG, BIG), BIG)

    start_group(
        "g1", lambda j: s["gb"].at[tap_rows(c_ranks[j])], lambda j: s["r1"].at[j], c_peers
    )

    arrive("wxy")
    unpack_xy(window, 2, s["wxr"], s["wyr"], s["wer"], flags)
    pack_z(window, 36, 2, s["wzs"])
    start_z("wz", s["wzs"], s["wzr"])

    arrive("wz")
    unpack_z(window, 36, 2, s["wzr"], flags)

    def keep(xi, z):
        press[xi + 1, 0:32, 0:128] = z

    local_solve(window, s["mask"], s["za"], s["zb"], flags, None, keep)
    start_xy(
        "pxy", press, 3, s["pxs"], s["pxr"], s["pys"], s["pyr"], s["pes"], s["per"]
    )

    gs = s["gs"]
    gs[...] = jnp.zeros((128, 128), F32)
    gs[82:88, :] = dot(error, deep, 0, 0)[0:6]
    hidden_gradient(dout, s["wp"], s["back"])
    gs[81:82, :] = norm_backward(s["back"], s["cen"], gain, rstd, s["dn"])
    first_gradient(sel, s["mx"], s["dn"], gs)
    s["gsb"][...] = gs[...].astype(BF16)
    small_copies = []
    for n in range(SMALL):
        owner = TAPS + n
        rows = slice(n * BIG, (n + 1) * BIG)
        copy = pltpu.make_async_remote_copy(
            src_ref=s["gsb"].at[rows],
            dst_ref=s["r1s"].at[c],
            send_sem=send_sem.at[GROUP_STEPS.index("s0") + n],
            recv_sem=recv_sem.at[GROUP_STEPS.index("s0")],
            device_id=device(owner // 2 * 16 + z * 2 + owner % 2),
            device_id_type=MESH,
        )
        small_copies.append((owner, copy))

        @pl.when(c != owner)
        def _(copy=copy):
            copy.start()

        @pl.when(c == owner)
        def _(rows=rows):
            s["r1s"][c] = s["gsb"][rows, :]

    arrive_group("g1", s["r1"].at[1:OWNERS], c_peers)
    total = s["gb"][tap_rows(c), :].astype(F32)
    for j in range(1, OWNERS):
        total = total + s["r1"][j].astype(F32)
    s["parts"][z] = total.astype(BF16)

    @pl.when((c == TAPS) | (c == TAPS + 1))
    def _():
        slots = s["r1s"].at[0 : OWNERS - 1]
        remote(GROUP_STEPS.index("s0"), slots, slots, c_peers[1]).wait_recv()
        total = s["r1s"][0].astype(F32)
        for q in range(1, OWNERS):
            total = total + s["r1s"][q].astype(F32)
        s["parts"][z] = total.astype(BF16)

    start_group("g2", lambda j: s["parts"].at[z], lambda j: s["parts"].at[z], z_peers)
    pred_ref[...] = dot(stress.astype(BF16), cell_order(), 0, 0)[0:8]

    arrive("pxy")
    unpack_xy(press, 3, s["pxr"], s["pyr"], s["per"], flags)
    pack_z(press, 38, 3, s["pzs"])
    start_z("pz", s["pzs"], s["pzr"])

    arrive_group("g2", s["parts"].at[0:7], z_peers)
    total = s["parts"][0].astype(F32)
    for q in range(1, 8):
        total = total + s["parts"][q].astype(F32)
    gathered = s["gathered"]
    gathered[c] = total.astype(BF16)
    start_group("g3", lambda j: gathered.at[c], lambda j: gathered.at[c], c_peers)

    arrive("pz")
    unpack_z(press, 38, 3, s["pzr"], flags)

    def finish(xi, z):
        s["done"][xi - 2] = press[xi + 1, 0:32, 0:128] + z

    local_solve(window, s["mask"], s["za"], s["zb"], flags, press, finish)
    store_pressure = pltpu.make_async_copy(s["done"], pressure_ref, local_sem.at[2])
    store_pressure.start()

    arrive_group("g3", gathered.at[0 : OWNERS - 1], c_peers)
    store_gradient = pltpu.make_async_copy(
        gathered.at[0 : TAPS + SMALL], grad_ref, local_sem.at[3]
    )
    store_gradient.start()
    for copies in flights.values():
        for copy in copies:
            copy.wait_send()
    for owner, copy in small_copies:

        @pl.when(c != owner)
        def _(copy=copy):
            copy.wait_send()

    store_pressure.wait()
    store_gradient.wait()


def finish_kernel(
    pressure_in, pred_in, grad_in, pressure_out, pred_out, first, gain, second, head, small_in
):
    small_in[...] = grad_in[TAPS : TAPS + SMALL].reshape(SMALL * BIG, 128).astype(F32)
    pressure_out[0] = pressure_in[...]
    for k in range(6):
        pred_out[0, :, lanes(k, 512)] = pred_in[k : k + 1, :].astype(BF16)
    for kx in range(3):
        for ky in range(3):
            for kz in range(3):
                k = (kx * 3 + ky) * 3 + kz
                second[kx, ky, kz] = grad_in[k].astype(F32)
                first[kx, ky, kz] = small_in[k * 3 : k * 3 + 3, 0:64]
    gain[...] = small_in[81:82, 0:64]
    head[...] = small_in[82:88, :]


def shards(
    velocity,
    first_kernel,
    norm_gain,
    second_kernel,
    head_weight,
    selection,
    assignment,
    target_stress,
):
    vmem = pl.BlockSpec(memory_space=pltpu.VMEM)
    smem = pl.BlockSpec(memory_space=pltpu.SMEM)
    anywhere = pl.BlockSpec(memory_space=pl.ANY)
    pressure, stress, grads = pl.pallas_call(
        kernel,
        out_shape=[
            jax.ShapeDtypeStruct((32, 32, 128), F32),
            jax.ShapeDtypeStruct((8, 512), F32),
            jax.ShapeDtypeStruct((TAPS + SMALL, BIG, 128), BF16),
        ],
        in_specs=[smem, smem, anywhere, vmem, vmem, anywhere, vmem, vmem],
        out_specs=[anywhere, vmem, anywhere],
        scratch_shapes=[pltpu.VMEM(shape, kind) for shape, kind in SCRATCH.values()]
        + [pltpu.SemaphoreType.DMA((n,)) for n in (SEMAPHORES, SEMAPHORES, 4)],
        compiler_params=pltpu.CompilerParams(
            collective_id=0, has_side_effects=True, vmem_limit_bytes=56 << 20
        ),
    )(
        selection,
        assignment.reshape(-1),
        velocity,
        first_kernel,
        norm_gain.reshape(1, 64),
        second_kernel,
        head_weight.T,
        target_stress,
    )
    pressure, predicted, first, gain, second, head = pl.pallas_call(
        finish_kernel,
        out_shape=[
            jax.ShapeDtypeStruct((1, 32, 32, 128), F32),
            jax.ShapeDtypeStruct((1, 1, 3072), BF16),
            jax.ShapeDtypeStruct((3, 3, 3, 3, 64), F32),
            jax.ShapeDtypeStruct((1, 64), F32),
            jax.ShapeDtypeStruct((3, 3, 3, 64, 128), F32),
            jax.ShapeDtypeStruct((6, 128), F32),
        ],
        in_specs=[vmem] * 3,
        out_specs=[vmem] * 6,
        scratch_shapes=[pltpu.VMEM((SMALL * BIG, 128), F32)],
    )(pressure, stress, grads)
    return (pressure, predicted, first, gain.reshape(64), second, head.T)


def solution(mesh):
    placed = (
        P(("sec", "dom"), None, None, None, None),
        P(),
        P(),
        P(),
        P(),
        P(("sec", "dom"), None),
        P(),
        P(("sec", "dom"), None, None),
    )
    return jax.shard_map(
        shards,
        mesh=mesh,
        in_specs=placed,
        out_specs=(
            P(("sec", "dom"), None, None, None),
            P(("sec", "dom"), None, None),
            P(),
            P(),
            P(),
            P(),
        ),
        check_vma=False,
    )
```
